32 devices in a mesh: grp: 2 (over core), reg: 16 (over z, y, x).
Axes of the slice: x: 2, y: 2, z: 4, core: 2. Of those that a mesh axis runs over, the one named last changes fastest.
Arguments:
- cam_jacobian: bfloat16 [18, 65536], P(None, ('grp', 'reg')), may hold values from -6 to 6
- point_jacobian: bfloat16 [6, 65536], P(None, ('grp', 'reg')), may hold values from -6 to 6
- residuals: float32 [2, 65536], P(None, ('grp', 'reg')), may hold values from -48 to 48
- obs_camera: int32 [65536], P(('grp', 'reg')), may hold values from 0 to 4095, as said below
- obs_point: int32 [65536], P(('grp', 'reg')), may hold values from 0 to 255
Outputs:
- cam_step: float32 [9, 4096], P(None, ('grp', 'reg'))
- point_step: float32 [3, 8192], P(None, ('grp', 'reg'))
The draws below stay inside these ranges and needn't reach their ends.
Inputs may be any that keep to these rules, and one draw needn't show every extreme that they name: `obs_camera`: an observation in block d of 2048 rows sees a camera of block e = camera // 128 such that d // (number of reg devices) and e // (number of reg devices) may differ, but d and e differ by at most one modulo the number of reg devices (the same, the previous or the next region, never across the ends); every such block is seen.
All inputs are finite; a program needn't handle non-finite values.
Results may differ from the reference program's by a relative error of at most 0.0003.
Values sent between devices are 32-bit elements; how exact they have to be, the bound alone decides.
A program may use at most 64 MiB of HBM per device.

```python
import math
import jax
import jax.numpy as jnp
import numpy as np
from jax import lax

C_DEV = 128
P_DEV = 256
OBS_DEV = 2048
ITERS = 3
CAMS = 4096
POINTS = 8192
OBSERVATIONS = 65536
N_REG = 16


def draw_obs_camera(key, part):
    rows_index = jnp.arange(OBSERVATIONS, dtype=jnp.int32)
    owner_block = rows_index // OBS_DEV
    region = owner_block % N_REG
    key_first, key_second, key_third = jax.random.split(key, 3)
    offset = jax.random.randint(key_first, (OBSERVATIONS,), -1, 2)
    target = region + offset
    target = jnp.where(target < 0, region + 1, jnp.where(target >= N_REG, region - 1, target))
    partner = jax.random.randint(key_second, (OBSERVATIONS,), 0, 2)
    column = jax.random.randint(key_third, (OBSERVATIONS,), 0, C_DEV)
    return ((partner * N_REG + target) * C_DEV + column).astype(jnp.int32)


def set_ends(array, stream_key, low, high):
    place = [jax.random.randint(jax.random.fold_in(stream_key, axis), (), 0, length) for axis, length in enumerate(array.shape)]
    longest = array.shape.index(max(array.shape))
    beside = place[:longest] + [(place[longest] + 1) % array.shape[longest]] + place[longest + 1:]
    return array.at[tuple(place)].set(low).at[tuple(beside)].set(high)


def block_scale(key, shape, cuts, smallest, top_value):
    level = 1.0
    for position, shards_of in cuts:
        steps = jax.random.uniform(jax.random.fold_in(jax.random.fold_in(key, 6), position), (shards_of,), jnp.float32, smallest / len(cuts), top_value / len(cuts))
        level = level * jnp.repeat(jnp.exp(steps), shape[position] // shards_of).reshape((-1,) + (1,) * (len(shape) - 1 - position))
    return level


def cumulative_ranks(count, lean):
    loads = [(1 << 20) // math.isqrt(standing ** lean) + 1 for standing in range(1, count + 1)]
    width = 1 + sum(loads) // (1 << 30)
    return np.cumsum(np.array([max(1, weight // width) for weight in loads]))


def ranked_ids(own_key, dims, count, skew):
    grid = cumulative_ranks(count, skew)
    pick = jax.random.randint(jax.random.fold_in(own_key, 1), dims, 0, int(grid[count - 1]))
    grade = jnp.searchsorted(jnp.asarray(grid, jnp.int32), pick, side="right")
    return jax.random.permutation(jax.random.fold_in(own_key, 2), count)[grade].astype(jnp.int32)


def gaussian(own_key, shape, deviation, limit, cuts=(), kind=jnp.bfloat16):
    factor_of = block_scale(own_key, shape, cuts, -0.22, 0.18) if cuts else 1.0
    entries = jax.random.normal(own_key, shape, jnp.float32) * deviation * factor_of
    return jnp.minimum(jnp.maximum(entries, -limit), limit).astype(kind)


def setup_inputs(seed: int = 0) -> dict:
    arg_keys = jax.random.split(jax.random.key(seed), 6)
    return {
        "cam_jacobian": gaussian(arg_keys[0], (18, OBSERVATIONS), 1.0, 6.0, ((1, 32),)),
        "point_jacobian": gaussian(arg_keys[1], (6, OBSERVATIONS), 1.0, 6.0, ((1, 32),)),
        "residuals": gaussian(arg_keys[2], (2, OBSERVATIONS), 8.0, 48.0, ((1, 32),), jnp.float32),
        "obs_camera": draw_obs_camera(jax.random.fold_in(arg_keys[5], 71), 0),
        "obs_point": set_ends(ranked_ids(arg_keys[4], (OBSERVATIONS,), P_DEV, 1), jax.random.fold_in(arg_keys[4], 3), 0, P_DEV - 1).astype(jnp.int32),
    }


DAMPING = 4.0

def inverse_three(matrix):
    a, b, c, d, e, f, g, h, i = [matrix[k] for k in range(9)]
    adjoint = [e * i - f * h, c * h - b * i, b * f - c * e, f * g - d * i, a * i - c * g, c * d - a * f, d * h - e * g, b * g - a * h, a * e - b * d]
    determinant = a * adjoint[0] + b * adjoint[3] + c * adjoint[6]
    return jnp.stack(adjoint) / determinant

def apply_three(inverse, vector):
    return jnp.stack([inverse[3 * i] * vector[0] + inverse[3 * i + 1] * vector[1] + inverse[3 * i + 2] * vector[2] for i in range(3)])

def cholesky_rows(blocks):
    factor = [[None] * 9 for i in range(9)]
    for i in range(9):
        for j in range(i + 1):
            total = blocks[9 * i + j]
            for k in range(j):
                total = total - factor[i][k] * factor[j][k]
            if i == j:
                factor[i][i] = jnp.sqrt(total)
            else:
                factor[i][j] = total / factor[j][j]
    return factor

def cholesky_apply(factor, right):
    forward = []
    for i in range(9):
        total = right[i]
        for k in range(i):
            total = total - factor[i][k] * forward[k]
        forward.append(total / factor[i][i])
    backward = [None] * 9
    for i in range(8, -1, -1):
        total = forward[i]
        for k in range(i + 1, 9):
            total = total - factor[k][i] * backward[k]
        backward[i] = total / factor[i][i]
    return jnp.stack(backward)

def eliminate(values, cam_rows, point_rows, point_slot, inverse, count):
    gathered = jnp.zeros((3, count), jnp.float32).at[:, point_slot].add(lax.optimization_barrier(jnp.sum(point_rows * values[:, None], 0)))
    solved = apply_three(inverse, gathered)
    remain = values - lax.optimization_barrier(jnp.sum(point_rows * solved[:, point_slot][None], 1))
    return lax.optimization_barrier(jnp.sum(cam_rows * remain[:, None], 0))

def reference(cam_jacobian, point_jacobian, residuals, obs_camera, obs_point):
    rows_index = jnp.arange(OBSERVATIONS, dtype=jnp.int32)
    point_slot = (obs_point + rows_index // OBS_DEV * P_DEV).astype(jnp.int32)
    cam_rows = cam_jacobian.astype(jnp.float32).reshape(2, 9, OBSERVATIONS)
    point_rows = point_jacobian.astype(jnp.float32).reshape(2, 3, OBSERVATIONS)
    pairs = lax.optimization_barrier(jnp.sum(point_rows[:, :, None] * point_rows[:, None, :], 0)).reshape(9, OBSERVATIONS)
    point_blocks = jnp.zeros((9, POINTS), jnp.float32).at[:, point_slot].add(pairs)
    point_blocks = point_blocks + DAMPING * jnp.eye(3, dtype=jnp.float32).reshape(9, 1)
    inverse = inverse_three(point_blocks)
    outer = lax.optimization_barrier(jnp.sum(cam_rows[:, :, None] * cam_rows[:, None, :], 0)).reshape(81, OBSERVATIONS)
    normal = jnp.zeros((81, CAMS), jnp.float32).at[:, obs_camera].add(outer)
    blocks = normal + DAMPING * jnp.eye(9, dtype=jnp.float32).reshape(81, 1)
    factor = cholesky_rows(blocks)
    right = -jnp.zeros((9, CAMS), jnp.float32).at[:, obs_camera].add(eliminate(residuals, cam_rows, point_rows, point_slot, inverse, POINTS))

    def reduced(direction):
        values = lax.optimization_barrier(jnp.sum(cam_rows * direction[:, obs_camera][None], 1))
        terms = eliminate(values, cam_rows, point_rows, point_slot, inverse, POINTS)
        return DAMPING * direction + jnp.zeros((9, CAMS), jnp.float32).at[:, obs_camera].add(terms)
    cam_step = jnp.zeros((9, CAMS), jnp.float32)
    residual = right
    precon = cholesky_apply(factor, residual)
    direction = precon
    current = jnp.sum(residual * precon)
    for turn in range(ITERS):
        product = reduced(direction)
        step_size = current / jnp.sum(direction * product)
        cam_step = cam_step + step_size * direction
        if turn + 1 < ITERS:
            residual = residual - step_size * product
            precon = cholesky_apply(factor, residual)
            following = jnp.sum(residual * precon)
            direction = precon + following / current * direction
            current = following
    values = residuals + lax.optimization_barrier(jnp.sum(cam_rows * cam_step[:, obs_camera][None], 1))
    gathered = jnp.zeros((3, POINTS), jnp.float32).at[:, point_slot].add(lax.optimization_barrier(jnp.sum(point_rows * values[:, None], 0)))
    point_step = -apply_three(inverse, gathered)
    return (cam_step, point_step)
```

```python
import functools

import jax
import jax.numpy as jnp
from jax import lax
from jax.experimental import pallas as pl
from jax.experimental.pallas import tpu as pltpu
from jax.sharding import PartitionSpec as P

C_DEV = 128
P_DEV = 256
ITERS = 3
DAMPING = 4.0

LANES = 128
ROWS = 16
PAIRS = [(i, j) for i in range(9) for j in range(i + 1)]
NORMAL_ROWS = 64
PARTS = 3
MESH = pl.DeviceIdType.MESH


def split(x):
    parts = []
    for _ in range(PARTS - 1):
        part = x.astype(jnp.bfloat16)
        parts.append(part)
        x = x - part.astype(jnp.float32)
    parts.append(x.astype(jnp.bfloat16))
    return jnp.concatenate(parts, 0)


def sum_into(terms, onehot):
    rows = terms.shape[0]
    summed = jnp.dot(split(terms), onehot, preferred_element_type=jnp.float32)
    total = summed[(PARTS - 1) * rows :]
    for part in range(PARTS - 2, -1, -1):
        total = total + summed[part * rows : (part + 1) * rows]
    return total


def inverse_three(a, b, c, e, f, i):
    adjoint = [e * i - f * f, c * f - b * i, b * f - c * e, a * i - c * c, b * c - a * f, a * e - b * b]
    determinant = a * adjoint[0] + b * adjoint[1] + c * adjoint[2]
    return [entry / determinant for entry in adjoint]


def apply_three(inverse, vector):
    a, b, c, e, f, i = inverse
    x, y, z = vector
    return [a * x + b * y + c * z, b * x + e * y + f * z, c * x + f * y + i * z]


def block_inverse(entry):
    factor = [[None] * 9 for _ in range(9)]
    scale = [None] * 9
    for j in range(9):
        total = entry(j, j)
        for k in range(j):
            total = total - factor[j][k] * factor[j][k]
        scale[j] = 1.0 / jnp.sqrt(total)
        for i in range(j + 1, 9):
            total = entry(i, j)
            for k in range(j):
                total = total - factor[i][k] * factor[j][k]
            factor[i][j] = total * scale[j]
    rows = lax.broadcasted_iota(jnp.int32, (ROWS, LANES), 0)
    forward = [jnp.where(rows == i, 1.0, 0.0) for i in range(9)]
    for i in range(9):
        forward[i] = forward[i] * scale[i]
        for k in range(i + 1, 9):
            forward[k] = forward[k] - factor[k][i] * forward[i]
    for i in range(8, -1, -1):
        forward[i] = forward[i] * scale[i]
        for k in range(i):
            forward[k] = forward[k] - factor[i][k] * forward[i]
    return forward


def kernel(
    groups,
    regions,
    cam_ref,
    point_ref,
    res_ref,
    camera_ref,
    slot_ref,
    cam_step_ref,
    point_step_ref,
    cam_rows,
    point_rows,
    residuals,
    cam_hot,
    point_hot,
    stage,
    normal_stage,
    normal_part,
    normal_recv,
    part,
    recv,
    table,
    scalars,
    near_send,
    near_recv,
    sum_send,
    sum_recv,
):
    group = lax.axis_index("grp")
    region = lax.axis_index("reg")
    devices = groups * regions
    me = group * regions + region
    blocks = 3 * groups
    tiles = camera_ref.shape[0]

    barrier = pltpu.get_barrier_semaphore()

    def greet(j, carry):
        other = lax.rem(me + j, devices)
        pl.semaphore_signal(
            barrier,
            inc=1,
            device_id=(other // regions, lax.rem(other, regions)),
            device_id_type=MESH,
        )
        return carry

    lax.fori_loop(1, devices, greet, 0)

    def near():
        peers = []
        for offset in range(3):
            other_region = lax.rem(region + offset - 1 + regions, regions)
            for j in range(1 if offset == 1 else 0, groups):
                other = lax.rem(group + j, groups)
                peers.append((offset * groups + other, (2 - offset) * groups + group, (other, other_region)))
        return peers

    peers = near()
    mine = groups + group

    def near_exchange(phase, source, target):
        copies = []
        for n, (block, slot, peer) in enumerate(peers):
            copy = pltpu.make_async_remote_copy(
                src_ref=source(block),
                dst_ref=target(slot),
                send_sem=near_send.at[phase, n],
                recv_sem=near_recv.at[phase, n],
                device_id=peer,
                device_id_type=MESH,
            )
            copy.start()
            copies.append(copy)
        return copies

    def sum_start(phase, row):
        scalars[phase, me] = row

        def push(j, carry):
            other = lax.rem(me + j, devices)
            pltpu.make_async_remote_copy(
                src_ref=scalars.at[phase, me],
                dst_ref=scalars.at[phase, me],
                send_sem=sum_send.at[phase],
                recv_sem=sum_recv.at[phase],
                device_id=(other // regions, lax.rem(other, regions)),
                device_id_type=MESH,
            ).start()
            return carry

        lax.fori_loop(1, devices, push, 0)

    def sum_wait(phase):
        bytes_of = scalars.at[phase, pl.ds(0, devices - 1)]
        pltpu.make_async_copy(bytes_of, bytes_of, sum_recv.at[phase]).wait()
        pltpu.make_async_copy(bytes_of, bytes_of, sum_send.at[phase]).wait()
        return jnp.sum(jnp.sum(scalars[phase], axis=0), axis=1, keepdims=True)

    for s in range(tiles):
        lanes = slice(s * LANES, (s + 1) * LANES)
        cam_rows[:, s, :] = cam_ref[:, lanes].astype(jnp.float32)
        point_rows[:, s, :] = point_ref[:, lanes].astype(jnp.float32)
        residuals[:, s, :] = res_ref[:, lanes]

    camera = camera_ref[...]
    owner = jnp.right_shift(camera, C_DEV.bit_length() - 1)
    lane = jnp.bitwise_and(camera, C_DEV - 1)
    owner_group = jnp.zeros_like(owner)
    for j in range(1, groups):
        owner_group = owner_group + jnp.where(owner >= j * regions, 1, 0)
    block_of = (owner - owner_group * regions - region + 1) * groups + owner_group
    slot = slot_ref[...]
    point_lane = jnp.bitwise_and(slot, LANES - 1)
    point_tile = jnp.right_shift(slot, LANES.bit_length() - 1)

    slot_t = jnp.transpose(slot.astype(jnp.float32))
    column_t = jnp.transpose((block_of * C_DEV + lane).astype(jnp.float32))
    point_iota = lax.broadcasted_iota(jnp.int32, (LANES, P_DEV), 1).astype(jnp.float32)
    cam_iota = lax.broadcasted_iota(jnp.int32, (LANES, blocks * C_DEV), 1).astype(jnp.float32)
    for s in range(tiles):
        at = slice(s * LANES, (s + 1) * LANES)
        point_hot[at, :] = jnp.where(slot_t[:, s : s + 1] == point_iota, 1.0, 0.0).astype(jnp.bfloat16)
        cam_hot[at, :] = jnp.where(column_t[:, s : s + 1] == cam_iota, 1.0, 0.0).astype(jnp.bfloat16)

    stage[...] = jnp.zeros_like(stage)
    normal_stage[...] = jnp.zeros_like(normal_stage)

    def staged(ref, rows):
        return jnp.concatenate([ref[s, :rows] for s in range(tiles)], 1)

    def pick(rows, tile, at):
        total = None
        for n, row in enumerate(rows):
            wide = jnp.broadcast_to(row, (tiles, LANES))
            got = jnp.take_along_axis(wide, at, axis=1, mode="promise_in_bounds")
            total = got if total is None else jnp.where(tile == n, got, total)
        return total

    def point_terms(values):
        for j in range(3):
            stage[:, j, :] = point_rows[j] * values[0] + point_rows[3 + j] * values[1]

    def rows_of(block, count):
        return [block[j : j + 1] for j in range(count)]

    def remains(values, gathered):
        solved = apply_three(inverse, rows_of(gathered, 3))
        picked = [
            pick([row[:, n * LANES : (n + 1) * LANES] for n in range(P_DEV // LANES)], point_tile, point_lane)
            for row in solved
        ]
        return [
            values[i]
            - (
                point_rows[3 * i] * picked[0]
                + point_rows[3 * i + 1] * picked[1]
                + point_rows[3 * i + 2] * picked[2]
            )
            for i in range(2)
        ]

    first = [residuals[0], residuals[1]]
    point_terms(first)
    for n, (i, j) in enumerate([(0, 0), (0, 1), (0, 2), (1, 1), (1, 2), (2, 2)]):
        stage[:, 3 + n, :] = point_rows[i] * point_rows[j] + point_rows[3 + i] * point_rows[3 + j]
    sums = sum_into(staged(stage, ROWS), point_hot[...])
    entries = rows_of(sums[3:9], 6)
    for n in (0, 3, 5):
        entries[n] = entries[n] + DAMPING
    inverse = inverse_three(*entries)
    point_total = sums[:8]

    remain = remains(first, sums)
    for n, (i, j) in enumerate(PAIRS):
        normal_stage[:, n, :] = cam_rows[i] * cam_rows[j] + cam_rows[9 + i] * cam_rows[9 + j]
    for k in range(9):
        normal_stage[:, 45 + k, :] = cam_rows[k] * remain[0] + cam_rows[9 + k] * remain[1]
    summed = sum_into(staged(normal_stage, NORMAL_ROWS), cam_hot[...])
    for n in range(blocks):
        normal_part[n] = summed[:, n * C_DEV : (n + 1) * C_DEV]
    pl.semaphore_wait(barrier, devices - 1)
    copies = near_exchange(0, lambda block: normal_part.at[block], lambda at: normal_recv.at[at])
    normal_recv[mine] = normal_part[mine]
    for copy in copies:
        copy.wait()
    total = normal_recv[0]
    for n in range(1, blocks):
        total = total + normal_recv[n]

    def entry(i, j):
        n = PAIRS.index((i, j))
        row = total[n : n + 1]
        return row + DAMPING if i == j else row

    solve = block_inverse(entry)
    live = lax.broadcasted_iota(jnp.int32, (ROWS, LANES), 0) < 9
    residual = jnp.where(live, -total[45 : 45 + ROWS], 0.0)

    def precondition(field):
        out = solve[0] * field[0:1]
        for k in range(1, 9):
            out = out + solve[k] * field[k : k + 1]
        return out

    cam_step = jnp.zeros((ROWS, LANES), jnp.float32)
    direction = current = values = gathered = None
    for turn in range(ITERS):
        precon = precondition(residual)
        table[turn, mine] = precon
        copies = near_exchange(
            1 + 2 * turn, lambda block: table.at[turn, mine], lambda at: table.at[turn, at]
        )
        sum_start(2 * turn, jnp.sum(residual * precon, axis=0, keepdims=True))
        for copy in copies:
            copy.wait()
        fresh = [None, None]
        for k in range(9):
            picked = pick([table[turn, n, k : k + 1] for n in range(blocks)], block_of, lane)
            for i in range(2):
                term = cam_rows[9 * i + k] * picked
                fresh[i] = term if k == 0 else fresh[i] + term
        point_terms(fresh)
        fresh_sums = sum_into(staged(stage, ROWS), point_hot[...])[:8]
        following = sum_wait(2 * turn)
        if turn == 0:
            values, gathered, direction = fresh, fresh_sums, precon
        else:
            ratio = following / current
            values = [fresh[i] + ratio * values[i] for i in range(2)]
            gathered = fresh_sums + ratio * gathered
            direction = precon + ratio * direction
        current = following
        remain = remains(values, gathered)
        energy = jnp.sum(values[0] * remain[0] + values[1] * remain[1], axis=0, keepdims=True)
        energy = energy + DAMPING * jnp.sum(direction * direction, axis=0, keepdims=True)
        sum_start(2 * turn + 1, energy)
        copies = []
        if turn + 1 < ITERS:
            for k in range(9):
                stage[:, k, :] = cam_rows[k] * remain[0] + cam_rows[9 + k] * remain[1]
            product = sum_into(staged(stage, ROWS), cam_hot[...])
            for n in range(blocks):
                part[turn, n] = product[:, n * C_DEV : (n + 1) * C_DEV]
            copies = near_exchange(
                2 + 2 * turn, lambda block: part.at[turn, block], lambda at: recv.at[turn, at]
            )
            recv[turn, mine] = part[turn, mine]
        step_size = current / sum_wait(2 * turn + 1)
        cam_step = cam_step + step_size * direction
        point_total = point_total + step_size * gathered
        if turn + 1 < ITERS:
            for copy in copies:
                copy.wait()
            image = DAMPING * direction
            for n in range(blocks):
                image = image + recv[turn, n]
            residual = jnp.where(live, residual - step_size * image, 0.0)

    cam_step_ref[...] = cam_step[:9]
    for j, row in enumerate(apply_three(inverse, rows_of(point_total, 3))):
        point_step_ref[j : j + 1, :] = -row


def local(groups, regions, cam_jacobian, point_jacobian, residuals, obs_camera, obs_point):
    count = obs_camera.shape[0]
    tiles = count // LANES
    blocks = 3 * groups
    devices = groups * regions
    phases = 2 * ITERS
    f32, bf16 = jnp.float32, jnp.bfloat16
    near = blocks - 1
    return pl.pallas_call(
        functools.partial(kernel, groups, regions),
        out_shape=(
            jax.ShapeDtypeStruct((9, C_DEV), f32),
            jax.ShapeDtypeStruct((3, P_DEV), f32),
        ),
        in_specs=[pl.BlockSpec(memory_space=pltpu.VMEM)] * 5,
        out_specs=[pl.BlockSpec(memory_space=pltpu.VMEM)] * 2,
        scratch_shapes=[
            pltpu.VMEM((18, tiles, LANES), f32),
            pltpu.VMEM((6, tiles, LANES), f32),
            pltpu.VMEM((2, tiles, LANES), f32),
            pltpu.VMEM((count, blocks * C_DEV), bf16),
            pltpu.VMEM((count, P_DEV), bf16),
            pltpu.VMEM((tiles, ROWS, LANES), f32),
            pltpu.VMEM((tiles, NORMAL_ROWS, LANES), f32),
            pltpu.VMEM((blocks, NORMAL_ROWS, C_DEV), f32),
            pltpu.VMEM((blocks, NORMAL_ROWS, C_DEV), f32),
            pltpu.VMEM((ITERS - 1, blocks, ROWS, C_DEV), f32),
            pltpu.VMEM((ITERS - 1, blocks, ROWS, C_DEV), f32),
            pltpu.VMEM((ITERS, blocks, ROWS, C_DEV), f32),
            pltpu.VMEM((phases, devices, 1, LANES), f32),
            pltpu.SemaphoreType.DMA((phases, near)),
            pltpu.SemaphoreType.DMA((phases, near)),
            pltpu.SemaphoreType.DMA((phases,)),
            pltpu.SemaphoreType.DMA((phases,)),
        ],
        compiler_params=pltpu.CompilerParams(
            collective_id=0, has_side_effects=True, vmem_limit_bytes=48 * 1024 * 1024
        ),
    )(
        cam_jacobian,
        point_jacobian,
        residuals,
        obs_camera.reshape(tiles, LANES),
        obs_point.reshape(tiles, LANES),
    )


def solution(mesh):
    placed = (
        P(None, ("grp", "reg")),
        P(None, ("grp", "reg")),
        P(None, ("grp", "reg")),
        P(("grp", "reg")),
        P(("grp", "reg")),
    )
    return jax.shard_map(
        functools.partial(local, mesh.shape["grp"], mesh.shape["reg"]),
        mesh=mesh,
        in_specs=placed,
        out_specs=(P(None, ("grp", "reg")), P(None, ("grp", "reg"))),
        check_vma=False,
    )
```

```python
import functools

import jax
import jax.numpy as jnp
from jax import lax
from jax.experimental import pallas as pl
from jax.experimental.pallas import tpu as pltpu
from jax.sharding import PartitionSpec as P

C_DEV = 128
P_DEV = 256
ITERS = 3
DAMPING = 4.0

LANES = 128
ROWS = 16
PAIRS = [(i, j) for i in range(9) for j in range(i + 1)]
NORMAL_ROWS = 56
PARTS = 3
MESH = pl.DeviceIdType.MESH


def split(x):
    parts = []
    for _ in range(PARTS - 1):
        part = x.astype(jnp.bfloat16).astype(jnp.float32)
        parts.append(part)
        x = x - part
    parts.append(x)
    return jnp.concatenate(parts, 0).astype(jnp.bfloat16)


def sum_into(terms, onehot):
    rows = terms.shape[0]
    summed = jnp.dot(split(terms), onehot, preferred_element_type=jnp.float32)
    total = summed[(PARTS - 1) * rows :]
    for part in range(PARTS - 2, -1, -1):
        total = total + summed[part * rows : (part + 1) * rows]
    return total


def inverse_three(a, b, c, e, f, i):
    adjoint = [e * i - f * f, c * f - b * i, b * f - c * e, a * i - c * c, b * c - a * f, a * e - b * b]
    determinant = a * adjoint[0] + b * adjoint[1] + c * adjoint[2]
    return [entry / determinant for entry in adjoint]


def apply_three(inverse, vector):
    a, b, c, e, f, i = inverse
    x, y, z = vector
    return [a * x + b * y + c * z, b * x + e * y + f * z, c * x + f * y + i * z]


def block_inverse(entry):
    work = {(i, j): entry(i, j) for i, j in PAIRS}
    for p in range(9):
        scale = 1.0 / work[p, p]
        column = [work[max(i, p), min(i, p)] for i in range(9)]
        scaled = [value * scale for value in column]
        for i, j in PAIRS:
            if i == p and j == p:
                work[i, j] = -scale
            elif i == p:
                work[i, j] = scaled[j]
            elif j == p:
                work[i, j] = scaled[i]
            else:
                work[i, j] = work[i, j] - column[i] * scaled[j]
    return work


def kernel(
    groups,
    regions,
    cam_in,
    point_in,
    res_in,
    camera_in,
    slot_in,
    cam_step_ref,
    point_step_ref,
    cam_ref,
    point_ref,
    res_ref,
    camera_ref,
    slot_ref,
    cam_rows,
    point_rows,
    residuals,
    cam_hot,
    point_hot,
    stage,
    wide_stage,
    normal_stage,
    solve,
    normal_part,
    normal_recv,
    part,
    recv,
    table,
    scalars,
    near_send,
    near_recv,
    sum_send,
    sum_recv,
    load,
):
    group = lax.axis_index("grp")
    region = lax.axis_index("reg")
    devices = groups * regions
    me = group * regions + region
    blocks = 3 * groups
    tiles = camera_ref.shape[0]

    loads = [
        pltpu.make_async_copy(source, target, load.at[n])
        for n, (source, target) in enumerate(
            [
                (camera_in, camera_ref),
                (slot_in, slot_ref),
                (cam_in, cam_ref),
                (point_in, point_ref),
                (res_in, res_ref),
            ]
        )
    ]
    for copy in loads:
        copy.start()

    def turned(position, step, size):
        return lax.select(position + step >= size, position + step - size, position + step)

    others_group = [turned(group, j, groups) for j in range(groups)]
    others_region = [turned(region, j, regions) for j in range(regions)]
    everyone = [(g, r) for r in others_region for g in others_group][1:]

    barrier = pltpu.get_barrier_semaphore()
    for other in everyone:
        pl.semaphore_signal(barrier, inc=1, device_id=other, device_id_type=MESH)

    def near():
        peers = []
        for offset in range(3):
            other_region = lax.rem(region + offset - 1 + regions, regions)
            for j in range(1 if offset == 1 else 0, groups):
                other = lax.rem(group + j, groups)
                peers.append((offset * groups + other, (2 - offset) * groups + group, (other, other_region)))
        return peers

    peers = near()
    mine = groups + group

    def near_exchange(phase, source, target):
        copies = []
        for n, (block, slot, peer) in enumerate(peers):
            copy = pltpu.make_async_remote_copy(
                src_ref=source(block),
                dst_ref=target(slot),
                send_sem=near_send.at[phase, n],
                recv_sem=near_recv.at[phase, n],
                device_id=peer,
                device_id_type=MESH,
            )
            copy.start()
            copies.append(copy)
        return copies

    def sum_start(phase, rows):
        scalars[phase, me] = jnp.concatenate(rows, 0)
        for other in everyone:
            pltpu.make_async_remote_copy(
                src_ref=scalars.at[phase, me],
                dst_ref=scalars.at[phase, me],
                send_sem=sum_send.at[phase],
                recv_sem=sum_recv.at[phase],
                device_id=other,
                device_id_type=MESH,
            ).start()

    def sum_wait(phase):
        bytes_of = scalars.at[phase, pl.ds(0, devices - 1)]
        pltpu.make_async_copy(bytes_of, bytes_of, sum_recv.at[phase]).wait()
        pltpu.make_async_copy(bytes_of, bytes_of, sum_send.at[phase]).wait()
        sums = jnp.sum(jnp.sum(scalars[phase], axis=0), axis=1, keepdims=True)
        return [sums[n : n + 1] for n in range(3)]

    stage[...] = jnp.zeros_like(stage)
    wide_stage[...] = jnp.zeros_like(wide_stage)
    normal_stage[...] = jnp.zeros_like(normal_stage)
    solve[...] = jnp.zeros_like(solve)

    for copy in loads[:2]:
        copy.wait()
    camera = camera_ref[...]
    owner = jnp.right_shift(camera, C_DEV.bit_length() - 1)
    lane = jnp.bitwise_and(camera, C_DEV - 1)
    owner_group = jnp.zeros_like(owner)
    for j in range(1, groups):
        owner_group = owner_group + jnp.where(owner >= j * regions, 1, 0)
    offset_of = owner - owner_group * regions - region + 1
    block_of = offset_of * groups + owner_group
    near_by = [offset_of == n for n in range(3)]
    slot = slot_ref[...]
    point_lane = jnp.bitwise_and(slot, LANES - 1)
    point_tile = jnp.right_shift(slot, LANES.bit_length() - 1)

    slot_t = jnp.transpose(slot.astype(jnp.float32))
    column_t = jnp.transpose((owner_group * C_DEV + lane).astype(jnp.float32))
    point_iota = lax.broadcasted_iota(jnp.int32, (LANES, P_DEV), 1).astype(jnp.float32)
    cam_iota = lax.broadcasted_iota(jnp.int32, (LANES, groups * C_DEV), 1).astype(jnp.float32)
    for s in range(tiles):
        at = slice(s * LANES, (s + 1) * LANES)
        point_hot[at, :] = jnp.where(slot_t[:, s : s + 1] == point_iota, 1.0, 0.0).astype(jnp.bfloat16)
        cam_hot[at, :] = jnp.where(column_t[:, s : s + 1] == cam_iota, 1.0, 0.0).astype(jnp.bfloat16)

    for copy in loads[2:]:
        copy.wait()
    for s in range(tiles):
        lanes = slice(s * LANES, (s + 1) * LANES)
        cam_rows[:, s, :] = cam_ref[:, lanes].astype(jnp.float32)
        point_rows[:, s, :] = point_ref[:, lanes].astype(jnp.float32)
        residuals[:, s, :] = res_ref[:, lanes]

    def staged(ref, rows):
        return jnp.concatenate([ref[s, :rows] for s in range(tiles)], 1)

    def pick(rows, tile, at):
        total = None
        for n, row in enumerate(rows):
            wide = jnp.broadcast_to(row, (tiles, LANES))
            got = jnp.take_along_axis(wide, at, axis=1, mode="promise_in_bounds")
            total = got if total is None else jnp.where(tile == n, got, total)
        return total

    def point_terms(values):
        for j in range(3):
            stage[:, j, :] = point_rows[j] * values[0] + point_rows[3 + j] * values[1]

    def place(ref, pitch, row, term):
        for n in range(3):
            ref[:, n * pitch + row, :] = jnp.where(near_by[n], term, 0.0)

    def by_block(ref, summed, pitch):
        for n in range(3):
            for j in range(groups):
                ref[n * groups + j] = summed[n * pitch : (n + 1) * pitch, j * C_DEV : (j + 1) * C_DEV]

    def rows_of(block, count):
        return [block[j : j + 1] for j in range(count)]

    def remains(values, gathered):
        solved = apply_three(inverse, rows_of(gathered, 3))
        picked = [
            pick([row[:, n * LANES : (n + 1) * LANES] for n in range(P_DEV // LANES)], point_tile, point_lane)
            for row in solved
        ]
        return [
            values[i]
            - (
                point_rows[3 * i] * picked[0]
                + point_rows[3 * i + 1] * picked[1]
                + point_rows[3 * i + 2] * picked[2]
            )
            for i in range(2)
        ]

    first = [residuals[0], residuals[1]]
    point_terms(first)
    for n, (i, j) in enumerate([(0, 0), (0, 1), (0, 2), (1, 1), (1, 2), (2, 2)]):
        stage[:, 3 + n, :] = point_rows[i] * point_rows[j] + point_rows[3 + i] * point_rows[3 + j]
    sums = sum_into(staged(stage, ROWS), point_hot[...])
    entries = rows_of(sums[3:9], 6)
    for n in (0, 3, 5):
        entries[n] = entries[n] + DAMPING
    inverse = inverse_three(*entries)
    point_total = sums[:8]

    remain = remains(first, sums)
    for n, (i, j) in enumerate(PAIRS):
        place(normal_stage, NORMAL_ROWS, n, cam_rows[i] * cam_rows[j] + cam_rows[9 + i] * cam_rows[9 + j])
    for k in range(9):
        place(normal_stage, NORMAL_ROWS, 45 + k, cam_rows[k] * remain[0] + cam_rows[9 + k] * remain[1])
    by_block(normal_part, sum_into(staged(normal_stage, 3 * NORMAL_ROWS), cam_hot[...]), NORMAL_ROWS)
    pl.semaphore_wait(barrier, devices - 1)
    copies = near_exchange(0, lambda block: normal_part.at[block], lambda at: normal_recv.at[at])
    normal_recv[mine] = normal_part[mine]
    for copy in copies:
        copy.wait()
    total = normal_recv[0]
    for n in range(1, blocks):
        total = total + normal_recv[n]

    def entry(i, j):
        n = PAIRS.index((i, j))
        row = total[n : n + 1]
        return row + DAMPING if i == j else row

    minus_inverse = block_inverse(entry)
    for i, j in PAIRS:
        solve[i, j : j + 1, :] = -minus_inverse[i, j]
        if i != j:
            solve[j, i : i + 1, :] = -minus_inverse[i, j]

    def precondition(field):
        out = solve[0] * field[0]
        for k in range(1, 9):
            out = out + solve[k] * field[k]
        return out

    def padded(rows):
        return jnp.concatenate(rows + [jnp.zeros((ROWS - 9, C_DEV), jnp.float32)], 0)

    residual = padded([-total[45:54]])
    cam_step = jnp.zeros((ROWS, C_DEV), jnp.float32)
    empty = jnp.zeros((5, C_DEV), jnp.float32)
    direction = image = gathered = current = curvature = None
    for turn in range(ITERS):
        precon = precondition([residual[k : k + 1] for k in range(9)])
        table[turn, mine] = precon
        copies = near_exchange(
            1 + 2 * turn, lambda block: table.at[turn, mine], lambda at: table.at[turn, at]
        )

        def dot(x, y):
            return jnp.sum(x * y, axis=0, keepdims=True)

        inner = dot(residual, precon)
        energy = DAMPING * dot(precon, precon)
        cross = jnp.zeros_like(inner) if turn == 0 else dot(precon, image)
        for copy in copies:
            copy.wait()
        values = [None, None]
        for k in range(9):
            picked = pick([table[turn, n, k : k + 1] for n in range(blocks)], block_of, lane)
            for i in range(2):
                term = cam_rows[9 * i + k] * picked
                values[i] = term if k == 0 else values[i] + term
        point_terms(values)
        fresh = sum_into(staged(stage, ROWS), point_hot[...])[:8]
        remain = remains(values, fresh)
        energy = energy + jnp.sum(values[0] * remain[0] + values[1] * remain[1], axis=0, keepdims=True)
        sum_start(turn, [inner, energy, cross, empty])
        last = turn + 1 == ITERS
        if not last:
            for k in range(9):
                place(wide_stage, ROWS, k, cam_rows[k] * remain[0] + cam_rows[9 + k] * remain[1])
            by_block(part.at[turn], sum_into(staged(wide_stage, 3 * ROWS), cam_hot[...]), ROWS)
            copies = near_exchange(
                2 + 2 * turn, lambda block: part.at[turn, block], lambda at: recv.at[turn, at]
            )
            recv[turn, mine] = part[turn, mine]
        following, energy, cross = sum_wait(turn)
        if turn == 0:
            curvature, direction, gathered = energy, precon, fresh
        else:
            ratio = following / current
            curvature = energy + ratio * (2.0 * cross + ratio * curvature)
            direction = precon + ratio * direction
            gathered = fresh + ratio * gathered
        current = following
        step_size = current / curvature
        cam_step = cam_step + step_size * direction
        point_total = point_total + step_size * gathered
        if not last:
            for copy in copies:
                copy.wait()
            product = DAMPING * precon
            for n in range(blocks):
                product = product + recv[turn, n]
            image = product if turn == 0 else product + ratio * image
            residual = residual - step_size * image

    cam_step_ref[...] = cam_step[:9]
    for j, row in enumerate(apply_three(inverse, rows_of(point_total, 3))):
        point_step_ref[j : j + 1, :] = -row


def local(groups, regions, cam_jacobian, point_jacobian, residuals, obs_camera, obs_point):
    count = obs_camera.shape[0]
    tiles = count // LANES
    blocks = 3 * groups
    devices = groups * regions
    phases = 2 * ITERS
    groups_wide = groups * C_DEV
    f32, bf16 = jnp.float32, jnp.bfloat16
    near = blocks - 1
    return pl.pallas_call(
        functools.partial(kernel, groups, regions),
        out_shape=(
            jax.ShapeDtypeStruct((9, C_DEV), f32),
            jax.ShapeDtypeStruct((3, P_DEV), f32),
        ),
        in_specs=[pl.BlockSpec(memory_space=pl.ANY)] * 5,
        out_specs=[pl.BlockSpec(memory_space=pltpu.VMEM)] * 2,
        scratch_shapes=[
            pltpu.VMEM(cam_jacobian.shape, bf16),
            pltpu.VMEM(point_jacobian.shape, bf16),
            pltpu.VMEM(residuals.shape, f32),
            pltpu.VMEM((tiles, LANES), jnp.int32),
            pltpu.VMEM((tiles, LANES), jnp.int32),
            pltpu.VMEM((18, tiles, LANES), f32),
            pltpu.VMEM((6, tiles, LANES), f32),
            pltpu.VMEM((2, tiles, LANES), f32),
            pltpu.VMEM((count, groups_wide), bf16),
            pltpu.VMEM((count, P_DEV), bf16),
            pltpu.VMEM((tiles, ROWS, LANES), f32),
            pltpu.VMEM((tiles, 3 * ROWS, LANES), f32),
            pltpu.VMEM((tiles, 3 * NORMAL_ROWS, LANES), f32),
            pltpu.VMEM((9, ROWS, C_DEV), f32),
            pltpu.VMEM((blocks, NORMAL_ROWS, C_DEV), f32),
            pltpu.VMEM((blocks, NORMAL_ROWS, C_DEV), f32),
            pltpu.VMEM((ITERS - 1, blocks, ROWS, C_DEV), f32),
            pltpu.VMEM((ITERS - 1, blocks, ROWS, C_DEV), f32),
            pltpu.VMEM((ITERS, blocks, ROWS, C_DEV), f32),
            pltpu.VMEM((ITERS, devices, 8, LANES), f32),
            pltpu.SemaphoreType.DMA((phases, near)),
            pltpu.SemaphoreType.DMA((phases, near)),
            pltpu.SemaphoreType.DMA((ITERS,)),
            pltpu.SemaphoreType.DMA((ITERS,)),
            pltpu.SemaphoreType.DMA((5,)),
        ],
        compiler_params=pltpu.CompilerParams(
            collective_id=0, has_side_effects=True, vmem_limit_bytes=48 * 1024 * 1024
        ),
    )(
        cam_jacobian,
        point_jacobian,
        residuals,
        obs_camera.reshape(tiles, LANES),
        obs_point.reshape(tiles, LANES),
    )


def solution(mesh):
    placed = (
        P(None, ("grp", "reg")),
        P(None, ("grp", "reg")),
        P(None, ("grp", "reg")),
        P(("grp", "reg")),
        P(("grp", "reg")),
    )
    return jax.shard_map(
        functools.partial(local, mesh.shape["grp"], mesh.shape["reg"]),
        mesh=mesh,
        in_specs=placed,
        out_specs=(P(None, ("grp", "reg")), P(None, ("grp", "reg"))),
        check_vma=False,
    )
```

```python
import functools

import jax
import jax.numpy as jnp
from jax import lax
from jax.experimental import pallas as pl
from jax.experimental.pallas import tpu as pltpu
from jax.sharding import PartitionSpec as P

C_DEV = 128
P_DEV = 256
ITERS = 3
DAMPING = 4.0

LANES = 128
ROWS = 16
PAIRS = [(i, j) for i in range(9) for j in range(i + 1)]
NORMAL_ROWS = 64
PARTS = 3
MESH = pl.DeviceIdType.MESH


def split(x):
    parts = []
    for _ in range(PARTS - 1):
        part = x.astype(jnp.bfloat16).astype(jnp.float32)
        parts.append(part)
        x = x - part
    parts.append(x)
    return jnp.concatenate(parts, 0).astype(jnp.bfloat16)


def sum_parts(summed):
    rows = summed.shape[0] // PARTS
    total = summed[(PARTS - 1) * rows :]
    for part in range(PARTS - 2, -1, -1):
        total = total + summed[part * rows : (part + 1) * rows]
    return total


def sum_into(terms, onehot):
    return sum_parts(jnp.dot(split(terms), onehot, preferred_element_type=jnp.float32))


def sum_near(terms, masks, onehot):
    parts = split(terms)
    masked = []
    for mask in masks:
        masked.append(parts * jnp.concatenate([mask] * (parts.shape[0] // mask.shape[0]), 0))
    summed = jnp.dot(jnp.concatenate(masked, 0), onehot, preferred_element_type=jnp.float32)
    rows = parts.shape[0]
    return [sum_parts(summed[n * rows : (n + 1) * rows]) for n in range(len(masks))]


def inverse_three(a, b, c, e, f, i):
    adjoint = [e * i - f * f, c * f - b * i, b * f - c * e, a * i - c * c, b * c - a * f, a * e - b * b]
    determinant = a * adjoint[0] + b * adjoint[1] + c * adjoint[2]
    return [entry / determinant for entry in adjoint]


def apply_three(inverse, vector):
    a, b, c, e, f, i = inverse
    x, y, z = vector
    return [a * x + b * y + c * z, b * x + e * y + f * z, c * x + f * y + i * z]


def block_inverse(entry):
    work = {(i, j): entry(i, j) for i, j in PAIRS}
    for p in range(9):
        scale = 1.0 / work[p, p]
        column = [work[max(i, p), min(i, p)] for i in range(9)]
        scaled = [value * scale for value in column]
        for i, j in PAIRS:
            if i == p and j == p:
                work[i, j] = -scale
            elif i == p:
                work[i, j] = scaled[j]
            elif j == p:
                work[i, j] = scaled[i]
            else:
                work[i, j] = work[i, j] - column[i] * scaled[j]
    return work


def kernel(
    groups,
    regions,
    cam_in,
    point_in,
    res_in,
    camera_in,
    slot_in,
    cam_step_ref,
    point_step_ref,
    cam_ref,
    point_ref,
    res_ref,
    camera_ref,
    slot_ref,
    cam_store,
    point_store,
    res_store,
    cam_hot,
    point_hot,
    stage,
    near_mask,
    normal_stage,
    solve,
    normal_part,
    normal_recv,
    part,
    recv,
    table,
    scalars,
    near_send,
    near_recv,
    sum_send,
    sum_recv,
    load,
):
    group = lax.axis_index("grp")
    region = lax.axis_index("reg")
    devices = groups * regions
    me = group * regions + region
    blocks = 3 * groups
    tiles = camera_ref.shape[0]

    loads = [
        pltpu.make_async_copy(source, target, load.at[n])
        for n, (source, target) in enumerate(
            [
                (camera_in, camera_ref),
                (slot_in, slot_ref),
                (cam_in, cam_ref),
                (point_in, point_ref),
                (res_in, res_ref),
            ]
        )
    ]
    for copy in loads:
        copy.start()

    def turned(position, step, size):
        return lax.select(position + step >= size, position + step - size, position + step)

    others_group = [turned(group, j, groups) for j in range(groups)]
    others_region = [turned(region, j, regions) for j in range(regions)]
    everyone = [(g, r) for r in others_region for g in others_group][1:]

    barrier = pltpu.get_barrier_semaphore()
    for other in everyone:
        pl.semaphore_signal(barrier, inc=1, device_id=other, device_id_type=MESH)

    def near():
        peers = []
        for offset in range(3):
            other_region = lax.rem(region + offset - 1 + regions, regions)
            for j in range(1 if offset == 1 else 0, groups):
                other = lax.rem(group + j, groups)
                peers.append((offset * groups + other, (2 - offset) * groups + group, (other, other_region)))
        return peers

    peers = near()
    mine = groups + group

    def near_exchange(phase, source, target):
        copies = []
        for n, (block, slot, peer) in enumerate(peers):
            copy = pltpu.make_async_remote_copy(
                src_ref=source(block),
                dst_ref=target(slot),
                send_sem=near_send.at[phase, n],
                recv_sem=near_recv.at[phase, n],
                device_id=peer,
                device_id_type=MESH,
            )
            copy.start()
            copies.append(copy)
        return copies

    def sum_start(phase, rows):
        scalars[phase, me] = jnp.concatenate(rows, 0)
        for other in everyone:
            pltpu.make_async_remote_copy(
                src_ref=scalars.at[phase, me],
                dst_ref=scalars.at[phase, me],
                send_sem=sum_send.at[phase],
                recv_sem=sum_recv.at[phase],
                device_id=other,
                device_id_type=MESH,
            ).start()

    def sum_wait(phase):
        bytes_of = scalars.at[phase, pl.ds(0, devices - 1)]
        pltpu.make_async_copy(bytes_of, bytes_of, sum_recv.at[phase]).wait()
        pltpu.make_async_copy(bytes_of, bytes_of, sum_send.at[phase]).wait()
        sums = jnp.sum(jnp.sum(scalars[phase], axis=0), axis=1, keepdims=True)
        return [sums[n : n + 1] for n in range(3)]

    stage[...] = jnp.zeros_like(stage)
    normal_stage[...] = jnp.zeros_like(normal_stage)
    solve[...] = jnp.zeros_like(solve)

    for copy in loads[:2]:
        copy.wait()
    camera = camera_ref[...]
    owner = jnp.right_shift(camera, C_DEV.bit_length() - 1)
    lane = jnp.bitwise_and(camera, C_DEV - 1)
    owner_group = jnp.zeros_like(owner)
    for j in range(1, groups):
        owner_group = owner_group + jnp.where(owner >= j * regions, 1, 0)
    offset_of = owner - owner_group * regions - region + 1
    block_of = offset_of * groups + owner_group
    for n in range(3):
        here = jnp.where(offset_of == n, 1.0, 0.0)
        for s in range(tiles):
            row = jnp.broadcast_to(here[s : s + 1], (ROWS, LANES))
            near_mask[n, :, s * LANES : (s + 1) * LANES] = row.astype(jnp.bfloat16)
    slot = slot_ref[...]
    point_lane = jnp.bitwise_and(slot, LANES - 1)
    point_tile = jnp.right_shift(slot, LANES.bit_length() - 1)

    slot_t = jnp.transpose(slot.astype(jnp.float32))
    column_t = jnp.transpose((owner_group * C_DEV + lane).astype(jnp.float32))
    point_iota = lax.broadcasted_iota(jnp.int32, (LANES, P_DEV), 1).astype(jnp.float32)
    cam_iota = lax.broadcasted_iota(jnp.int32, (LANES, groups * C_DEV), 1).astype(jnp.float32)
    for s in range(tiles):
        at = slice(s * LANES, (s + 1) * LANES)
        point_hot[at, :] = jnp.where(slot_t[:, s : s + 1] == point_iota, 1.0, 0.0).astype(jnp.bfloat16)
        cam_hot[at, :] = jnp.where(column_t[:, s : s + 1] == cam_iota, 1.0, 0.0).astype(jnp.bfloat16)

    for copy in loads[2:]:
        copy.wait()
    for s in range(tiles):
        lanes = slice(s * LANES, (s + 1) * LANES)
        cam_store[pl.ds(s, 18, stride=tiles), :] = cam_ref[:, lanes].astype(jnp.float32)
        point_store[pl.ds(s, 6, stride=tiles), :] = point_ref[:, lanes].astype(jnp.float32)
        res_store[pl.ds(s, 2, stride=tiles), :] = res_ref[:, lanes]
    cam_rows = [cam_store[n * tiles : (n + 1) * tiles] for n in range(18)]
    point_rows = [point_store[n * tiles : (n + 1) * tiles] for n in range(6)]
    residuals = [res_store[n * tiles : (n + 1) * tiles] for n in range(2)]

    def put(ref, row, term):
        ref[pl.ds(row, tiles, stride=ref.shape[0] // tiles), :] = term

    def staged(ref):
        rows = ref.shape[0] // tiles
        return jnp.concatenate([ref[s * rows : (s + 1) * rows] for s in range(tiles)], 1)

    def pick(rows, tile, at):
        total = None
        for n, row in enumerate(rows):
            wide = jnp.broadcast_to(row, (tiles, LANES))
            got = jnp.take_along_axis(wide, at, axis=1, mode="promise_in_bounds")
            total = got if total is None else jnp.where(tile == n, got, total)
        return total

    def point_terms(values):
        for j in range(3):
            put(stage, j, point_rows[j] * values[0] + point_rows[3 + j] * values[1])

    masks = [near_mask.at[n] for n in range(3)]

    def by_block(ref, summed):
        for n in range(3):
            for j in range(groups):
                ref[n * groups + j] = summed[n][:, j * C_DEV : (j + 1) * C_DEV]

    def rows_of(block, count):
        return [block[j : j + 1] for j in range(count)]

    def remains(values, gathered):
        solved = apply_three(inverse, rows_of(gathered, 3))
        picked = [
            pick([row[:, n * LANES : (n + 1) * LANES] for n in range(P_DEV // LANES)], point_tile, point_lane)
            for row in solved
        ]
        return [
            values[i]
            - (
                point_rows[3 * i] * picked[0]
                + point_rows[3 * i + 1] * picked[1]
                + point_rows[3 * i + 2] * picked[2]
            )
            for i in range(2)
        ]

    first = [residuals[0], residuals[1]]
    point_terms(first)
    for n, (i, j) in enumerate([(0, 0), (0, 1), (0, 2), (1, 1), (1, 2), (2, 2)]):
        put(stage, 3 + n, point_rows[i] * point_rows[j] + point_rows[3 + i] * point_rows[3 + j])
    sums = sum_into(staged(stage), point_hot[...])
    entries = rows_of(sums[3:9], 6)
    for n in (0, 3, 5):
        entries[n] = entries[n] + DAMPING
    inverse = inverse_three(*entries)
    point_total = sums[:8]

    remain = remains(first, sums)
    for n, (i, j) in enumerate(PAIRS):
        put(normal_stage, n, cam_rows[i] * cam_rows[j] + cam_rows[9 + i] * cam_rows[9 + j])
    for k in range(9):
        put(normal_stage, 45 + k, cam_rows[k] * remain[0] + cam_rows[9 + k] * remain[1])
    by_block(normal_part, sum_near(staged(normal_stage), [mask[...] for mask in masks], cam_hot[...]))
    pl.semaphore_wait(barrier, devices - 1)
    copies = near_exchange(0, lambda block: normal_part.at[block], lambda at: normal_recv.at[at])
    normal_recv[mine] = normal_part[mine]
    for copy in copies:
        copy.wait()
    total = normal_recv[0]
    for n in range(1, blocks):
        total = total + normal_recv[n]

    def entry(i, j):
        n = PAIRS.index((i, j))
        row = total[n : n + 1]
        return row + DAMPING if i == j else row

    minus_inverse = block_inverse(entry)
    for i, j in PAIRS:
        solve[i, j : j + 1, :] = -minus_inverse[i, j]
        if i != j:
            solve[j, i : i + 1, :] = -minus_inverse[i, j]

    def precondition(field):
        out = solve[0] * field[0]
        for k in range(1, 9):
            out = out + solve[k] * field[k]
        return out

    def padded(rows):
        return jnp.concatenate(rows + [jnp.zeros((ROWS - 9, C_DEV), jnp.float32)], 0)

    residual = padded([-total[45:54]])
    cam_step = jnp.zeros((ROWS, C_DEV), jnp.float32)
    empty = jnp.zeros((5, C_DEV), jnp.float32)
    direction = image = gathered = current = curvature = None
    for turn in range(ITERS):
        precon = precondition([residual[k : k + 1] for k in range(9)])
        table[turn, mine] = precon
        copies = near_exchange(
            1 + 2 * turn, lambda block: table.at[turn, mine], lambda at: table.at[turn, at]
        )

        def dot(x, y):
            return jnp.sum(x * y, axis=0, keepdims=True)

        inner = dot(residual, precon)
        energy = DAMPING * dot(precon, precon)
        cross = jnp.zeros_like(inner) if turn == 0 else dot(precon, image)
        for copy in copies:
            copy.wait()
        values = [None, None]
        for k in range(9):
            picked = pick([table[turn, n, k : k + 1] for n in range(blocks)], block_of, lane)
            for i in range(2):
                term = cam_rows[9 * i + k] * picked
                values[i] = term if k == 0 else values[i] + term
        point_terms(values)
        fresh = sum_into(staged(stage), point_hot[...])[:8]
        remain = remains(values, fresh)
        energy = energy + jnp.sum(values[0] * remain[0] + values[1] * remain[1], axis=0, keepdims=True)
        sum_start(turn, [inner, energy, cross, empty])
        last = turn + 1 == ITERS
        if not last:
            for k in range(9):
                put(stage, k, cam_rows[k] * remain[0] + cam_rows[9 + k] * remain[1])
            by_block(part.at[turn], sum_near(staged(stage), [mask[...] for mask in masks], cam_hot[...]))
            copies = near_exchange(
                2 + 2 * turn, lambda block: part.at[turn, block], lambda at: recv.at[turn, at]
            )
            recv[turn, mine] = part[turn, mine]
        following, energy, cross = sum_wait(turn)
        if turn == 0:
            curvature, direction, gathered = energy, precon, fresh
        else:
            ratio = following / current
            curvature = energy + ratio * (2.0 * cross + ratio * curvature)
            direction = precon + ratio * direction
            gathered = fresh + ratio * gathered
        current = following
        step_size = current / curvature
        cam_step = cam_step + step_size * direction
        point_total = point_total + step_size * gathered
        if not last:
            for copy in copies:
                copy.wait()
            product = DAMPING * precon
            for n in range(blocks):
                product = product + recv[turn, n]
            image = product if turn == 0 else product + ratio * image
            residual = residual - step_size * image

    cam_step_ref[...] = cam_step[:9]
    for j, row in enumerate(apply_three(inverse, rows_of(point_total, 3))):
        point_step_ref[j : j + 1, :] = -row


def local(groups, regions, cam_jacobian, point_jacobian, residuals, obs_camera, obs_point):
    count = obs_camera.shape[0]
    tiles = count // LANES
    blocks = 3 * groups
    devices = groups * regions
    phases = 2 * ITERS
    groups_wide = groups * C_DEV
    f32, bf16 = jnp.float32, jnp.bfloat16
    near = blocks - 1
    return pl.pallas_call(
        functools.partial(kernel, groups, regions),
        out_shape=(
            jax.ShapeDtypeStruct((9, C_DEV), f32),
            jax.ShapeDtypeStruct((3, P_DEV), f32),
        ),
        in_specs=[pl.BlockSpec(memory_space=pl.ANY)] * 5,
        out_specs=[pl.BlockSpec(memory_space=pltpu.VMEM)] * 2,
        scratch_shapes=[
            pltpu.VMEM(cam_jacobian.shape, bf16),
            pltpu.VMEM(point_jacobian.shape, bf16),
            pltpu.VMEM(residuals.shape, f32),
            pltpu.VMEM((tiles, LANES), jnp.int32),
            pltpu.VMEM((tiles, LANES), jnp.int32),
            pltpu.VMEM((18 * tiles, LANES), f32),
            pltpu.VMEM((6 * tiles, LANES), f32),
            pltpu.VMEM((2 * tiles, LANES), f32),
            pltpu.VMEM((count, groups_wide), bf16),
            pltpu.VMEM((count, P_DEV), bf16),
            pltpu.VMEM((tiles * ROWS, LANES), f32),
            pltpu.VMEM((3, ROWS, count), bf16),
            pltpu.VMEM((tiles * NORMAL_ROWS, LANES), f32),
            pltpu.VMEM((9, ROWS, C_DEV), f32),
            pltpu.VMEM((blocks, NORMAL_ROWS, C_DEV), f32),
            pltpu.VMEM((blocks, NORMAL_ROWS, C_DEV), f32),
            pltpu.VMEM((ITERS - 1, blocks, ROWS, C_DEV), f32),
            pltpu.VMEM((ITERS - 1, blocks, ROWS, C_DEV), f32),
            pltpu.VMEM((ITERS, blocks, ROWS, C_DEV), f32),
            pltpu.VMEM((ITERS, devices, 8, LANES), f32),
            pltpu.SemaphoreType.DMA((phases, near)),
            pltpu.SemaphoreType.DMA((phases, near)),
            pltpu.SemaphoreType.DMA((ITERS,)),
            pltpu.SemaphoreType.DMA((ITERS,)),
            pltpu.SemaphoreType.DMA((5,)),
        ],
        compiler_params=pltpu.CompilerParams(
            collective_id=0, has_side_effects=True, vmem_limit_bytes=48 * 1024 * 1024
        ),
    )(
        cam_jacobian,
        point_jacobian,
        residuals,
        obs_camera.reshape(tiles, LANES),
        obs_point.reshape(tiles, LANES),
    )


def solution(mesh):
    placed = (
        P(None, ("grp", "reg")),
        P(None, ("grp", "reg")),
        P(None, ("grp", "reg")),
        P(("grp", "reg")),
        P(("grp", "reg")),
    )
    return jax.shard_map(
        functools.partial(local, mesh.shape["grp"], mesh.shape["reg"]),
        mesh=mesh,
        in_specs=placed,
        out_specs=(P(None, ("grp", "reg")), P(None, ("grp", "reg"))),
        check_vma=False,
    )
```

```python
import functools

import jax
import jax.numpy as jnp
from jax import lax
from jax.experimental import pallas as pl
from jax.experimental.pallas import tpu as pltpu
from jax.sharding import PartitionSpec as P

C_DEV = 128
P_DEV = 256
ITERS = 3
DAMPING = 4.0

LANES = 128
ROWS = 16
PAIRS = [(i, j) for i in range(9) for j in range(i + 1)]
NORMAL_ROWS = 64
PARTS = 3
MESH = pl.DeviceIdType.MESH


def split(x):
    parts = []
    for _ in range(PARTS - 1):
        part = x.astype(jnp.bfloat16).astype(jnp.float32)
        parts.append(part)
        x = x - part
    parts.append(x)
    return jnp.concatenate(parts, 0).astype(jnp.bfloat16)


def sum_parts(summed):
    rows = summed.shape[0] // PARTS
    total = summed[(PARTS - 1) * rows :]
    for part in range(PARTS - 2, -1, -1):
        total = total + summed[part * rows : (part + 1) * rows]
    return total


def sum_into(terms, onehot):
    return sum_parts(jnp.dot(split(terms), onehot, preferred_element_type=jnp.float32))


def sum_near(terms, masks, onehot):
    parts = split(terms)
    masked = []
    for mask in masks:
        masked.append(parts * jnp.concatenate([mask] * (parts.shape[0] // mask.shape[0]), 0))
    summed = jnp.dot(jnp.concatenate(masked, 0), onehot, preferred_element_type=jnp.float32)
    rows = parts.shape[0]
    return [sum_parts(summed[n * rows : (n + 1) * rows]) for n in range(len(masks))]


def inverse_three(a, b, c, e, f, i):
    adjoint = [e * i - f * f, c * f - b * i, b * f - c * e, a * i - c * c, b * c - a * f, a * e - b * b]
    determinant = a * adjoint[0] + b * adjoint[1] + c * adjoint[2]
    return [entry / determinant for entry in adjoint]


def apply_three(inverse, vector):
    a, b, c, e, f, i = inverse
    x, y, z = vector
    return [a * x + b * y + c * z, b * x + e * y + f * z, c * x + f * y + i * z]


def block_inverse(entry):
    work = {(i, j): entry(i, j) for i, j in PAIRS}
    for p in range(9):
        scale = 1.0 / work[p, p]
        column = [work[max(i, p), min(i, p)] for i in range(9)]
        scaled = [value * scale for value in column]
        for i, j in PAIRS:
            if i == p and j == p:
                work[i, j] = -scale
            elif i == p:
                work[i, j] = scaled[j]
            elif j == p:
                work[i, j] = scaled[i]
            else:
                work[i, j] = work[i, j] - column[i] * scaled[j]
    return work


def inner_regions(regions):
    return max(n for n in range(1, regions + 1) if regions % n == 0 and n * n <= regions)


def kernel(
    groups,
    regions,
    cam_in,
    point_in,
    res_in,
    camera_in,
    slot_in,
    cam_step_ref,
    point_step_ref,
    cam_ref,
    point_ref,
    res_ref,
    camera_ref,
    slot_ref,
    cam_store,
    point_store,
    res_store,
    cam_hot,
    point_hot,
    stage,
    near_mask,
    normal_stage,
    solve,
    normal_part,
    normal_recv,
    part,
    recv,
    table,
    first_sums,
    second_sums,
    near_send,
    near_recv,
    sum_send,
    sum_recv,
    load,
):
    group = lax.axis_index("grp")
    region = lax.axis_index("reg")
    blocks = 3 * groups
    tiles = camera_ref.shape[0]

    loads = [
        pltpu.make_async_copy(source, target, load.at[n])
        for n, (source, target) in enumerate(
            [
                (camera_in, camera_ref),
                (slot_in, slot_ref),
                (cam_in, cam_ref),
                (point_in, point_ref),
                (res_in, res_ref),
            ]
        )
    ]
    for copy in loads:
        copy.start()

    def turned(position, step, size):
        return lax.select(position + step >= size, position + step - size, position + step)

    inner = inner_regions(regions)
    outer = regions // inner
    within = lax.rem(region, inner)
    plane = region // inner
    others_group = [turned(group, j, groups) for j in range(groups)]
    others_within = [turned(within, j, inner) for j in range(inner)]
    others_plane = [turned(plane, j, outer) for j in range(outer)]
    first_level = [(g, plane * inner + r) for r in others_within for g in others_group][1:]
    second_level = [(group, p * inner + within) for p in others_plane][1:]
    first_me = group * inner + within
    beside = [(g, turned(region, step, regions)) for step in (1, regions - 1) for g in others_group]

    barrier = pltpu.get_barrier_semaphore()
    for other in first_level + second_level + beside:
        pl.semaphore_signal(barrier, inc=1, device_id=other, device_id_type=MESH)
    greeted = len(first_level) + len(second_level) + len(beside)

    mine = groups + group
    has_below, has_above = region > 0, region < regions - 1

    class Near:
        def __init__(self, phase, source, target):
            self.copies = [[], [], []]
            n = 0
            for offset in range(3):
                for j in range(1 if offset == 1 else 0, groups):
                    other = others_group[j]
                    self.copies[offset].append(
                        pltpu.make_async_remote_copy(
                            src_ref=source(offset * groups + other),
                            dst_ref=target((2 - offset) * groups + group),
                            send_sem=near_send.at[phase, n],
                            recv_sem=near_recv.at[phase, n],
                            device_id=(other, turned(region, (offset - 1) % regions, regions)),
                            device_id_type=MESH,
                        )
                    )
                    n += 1

        def each(self, below, above, act):
            @pl.when(has_below)
            def _():
                for copy in self.copies[below]:
                    act(copy)

            @pl.when(has_above)
            def _():
                for copy in self.copies[above]:
                    act(copy)

            for copy in self.copies[1]:
                act(copy)

        def start(self):
            self.each(0, 2, lambda copy: copy.start())
            return self

        def wait(self):
            self.each(2, 0, lambda copy: copy.wait_recv())

        def finish(self):
            self.each(0, 2, lambda copy: copy.wait_send())

    def clear_ends(ref):
        @pl.when(region == 0)
        def _():
            for j in range(groups):
                ref[j] = jnp.zeros(ref.shape[1:], jnp.float32)

        @pl.when(region == regions - 1)
        def _():
            for j in range(groups):
                ref[2 * groups + j] = jnp.zeros(ref.shape[1:], jnp.float32)

    def push(ref, at, others, level, phase):
        for other in others:
            pltpu.make_async_remote_copy(
                src_ref=ref.at[phase, at],
                dst_ref=ref.at[phase, at],
                send_sem=sum_send.at[level, phase],
                recv_sem=sum_recv.at[level, phase],
                device_id=other,
                device_id_type=MESH,
            ).start()

    def pulled(ref, count, level, phase):
        bytes_of = ref.at[phase, pl.ds(0, count)]
        pltpu.make_async_copy(bytes_of, bytes_of, sum_recv.at[level, phase]).wait()
        return jnp.sum(ref[phase], axis=0)

    def sum_start(phase, row):
        first_sums[phase, first_me] = row
        push(first_sums, first_me, first_level, 0, phase)

    def sum_middle(phase):
        second_sums[phase, plane] = pulled(first_sums, len(first_level), 0, phase)
        push(second_sums, plane, second_level, 1, phase)

    def sum_wait(phase):
        sums = pulled(second_sums, len(second_level), 1, phase)
        return [sums[:, n : n + 1] for n in range(3)]

    def sum_finish(phase):
        for level, (ref, others) in enumerate([(first_sums, first_level), (second_sums, second_level)]):
            bytes_of = ref.at[phase, pl.ds(0, len(others))]
            pltpu.make_async_copy(bytes_of, bytes_of, sum_send.at[level, phase]).wait()

    clear_ends(normal_recv)
    for turn in range(ITERS):
        clear_ends(table.at[turn])
    for turn in range(ITERS - 1):
        clear_ends(recv.at[turn])
    stage[...] = jnp.zeros_like(stage)
    normal_stage[...] = jnp.zeros_like(normal_stage)
    solve[...] = jnp.zeros_like(solve)

    for copy in loads[:2]:
        copy.wait()
    camera = camera_ref[...]
    owner = jnp.right_shift(camera, C_DEV.bit_length() - 1)
    lane = jnp.bitwise_and(camera, C_DEV - 1)
    owner_group = jnp.zeros_like(owner)
    for j in range(1, groups):
        owner_group = owner_group + jnp.where(owner >= j * regions, 1, 0)
    offset_of = owner - owner_group * regions - region + 1
    block_of = offset_of * groups + owner_group
    for n in range(3):
        here = jnp.where(offset_of == n, 1.0, 0.0)
        for s in range(tiles):
            row = jnp.broadcast_to(here[s : s + 1], (ROWS, LANES))
            near_mask[n, :, s * LANES : (s + 1) * LANES] = row.astype(jnp.bfloat16)
    slot = slot_ref[...]
    point_lane = jnp.bitwise_and(slot, LANES - 1)
    point_tile = jnp.right_shift(slot, LANES.bit_length() - 1)

    slot_t = jnp.transpose(slot.astype(jnp.float32))
    column_t = jnp.transpose((owner_group * C_DEV + lane).astype(jnp.float32))
    point_iota = lax.broadcasted_iota(jnp.int32, (LANES, P_DEV), 1).astype(jnp.float32)
    cam_iota = lax.broadcasted_iota(jnp.int32, (LANES, groups * C_DEV), 1).astype(jnp.float32)
    for s in range(tiles):
        at = slice(s * LANES, (s + 1) * LANES)
        point_hot[at, :] = jnp.where(slot_t[:, s : s + 1] == point_iota, 1.0, 0.0).astype(jnp.bfloat16)
        cam_hot[at, :] = jnp.where(column_t[:, s : s + 1] == cam_iota, 1.0, 0.0).astype(jnp.bfloat16)

    for copy in loads[2:]:
        copy.wait()
    for s in range(tiles):
        lanes = slice(s * LANES, (s + 1) * LANES)
        cam_store[pl.ds(s, 18, stride=tiles), :] = cam_ref[:, lanes].astype(jnp.float32)
        point_store[pl.ds(s, 6, stride=tiles), :] = point_ref[:, lanes].astype(jnp.float32)
        res_store[pl.ds(s, 2, stride=tiles), :] = res_ref[:, lanes]
    cam_rows = [cam_store[n * tiles : (n + 1) * tiles] for n in range(18)]
    point_rows = [point_store[n * tiles : (n + 1) * tiles] for n in range(6)]
    residuals = [res_store[n * tiles : (n + 1) * tiles] for n in range(2)]

    def put(ref, row, term):
        ref[pl.ds(row, tiles, stride=ref.shape[0] // tiles), :] = term

    def staged(ref):
        rows = ref.shape[0] // tiles
        return jnp.concatenate([ref[s * rows : (s + 1) * rows] for s in range(tiles)], 1)

    def pick(rows, tile, at):
        total = None
        for n, row in enumerate(rows):
            wide = jnp.broadcast_to(row, (tiles, LANES))
            got = jnp.take_along_axis(wide, at, axis=1, mode="promise_in_bounds")
            total = got if total is None else jnp.where(tile == n, got, total)
        return total

    def point_terms(values):
        for j in range(3):
            put(stage, j, point_rows[j] * values[0] + point_rows[3 + j] * values[1])

    masks = [near_mask.at[n] for n in range(3)]

    def by_block(ref, summed):
        for n in range(3):
            for j in range(groups):
                ref[n * groups + j] = summed[n][:, j * C_DEV : (j + 1) * C_DEV]

    def rows_of(block, count):
        return [block[j : j + 1] for j in range(count)]

    def remains(values, gathered):
        solved = apply_three(inverse, rows_of(gathered, 3))
        picked = [
            pick([row[:, n * LANES : (n + 1) * LANES] for n in range(P_DEV // LANES)], point_tile, point_lane)
            for row in solved
        ]
        return [
            values[i]
            - (
                point_rows[3 * i] * picked[0]
                + point_rows[3 * i + 1] * picked[1]
                + point_rows[3 * i + 2] * picked[2]
            )
            for i in range(2)
        ]

    first = [residuals[0], residuals[1]]
    point_terms(first)
    for n, (i, j) in enumerate([(0, 0), (0, 1), (0, 2), (1, 1), (1, 2), (2, 2)]):
        put(stage, 3 + n, point_rows[i] * point_rows[j] + point_rows[3 + i] * point_rows[3 + j])
    sums = sum_into(staged(stage), point_hot[...])
    entries = rows_of(sums[3:9], 6)
    for n in (0, 3, 5):
        entries[n] = entries[n] + DAMPING
    inverse = inverse_three(*entries)
    point_total = sums[:8]

    remain = remains(first, sums)
    for n, (i, j) in enumerate(PAIRS):
        put(normal_stage, n, cam_rows[i] * cam_rows[j] + cam_rows[9 + i] * cam_rows[9 + j])
    for k in range(9):
        put(normal_stage, 45 + k, cam_rows[k] * remain[0] + cam_rows[9 + k] * remain[1])
    by_block(normal_part, sum_near(staged(normal_stage), [mask[...] for mask in masks], cam_hot[...]))
    pl.semaphore_wait(barrier, greeted)
    normal = Near(0, lambda block: normal_part.at[block], lambda at: normal_recv.at[at]).start()
    normal_recv[mine] = normal_part[mine]
    normal.wait()
    total = normal_recv[0]
    for n in range(1, blocks):
        total = total + normal_recv[n]

    def entry(i, j):
        n = PAIRS.index((i, j))
        row = total[n : n + 1]
        return row + DAMPING if i == j else row

    minus_inverse = block_inverse(entry)
    for i, j in PAIRS:
        solve[i, j : j + 1, :] = -minus_inverse[i, j]
        if i != j:
            solve[j, i : i + 1, :] = -minus_inverse[i, j]

    def precondition(field):
        out = solve[0] * field[0]
        for k in range(1, 9):
            out = out + solve[k] * field[k]
        return out

    def padded(rows):
        return jnp.concatenate(rows + [jnp.zeros((ROWS - 9, C_DEV), jnp.float32)], 0)

    residual = padded([-total[45:54]])
    cam_step = jnp.zeros((ROWS, C_DEV), jnp.float32)
    direction = image = gathered = current = curvature = None
    exchanges = []
    for turn in range(ITERS):
        precon = precondition([residual[k : k + 1] for k in range(9)])
        table[turn, mine] = precon
        spread = Near(
            1 + 2 * turn, lambda block: table.at[turn, mine], lambda at: table.at[turn, at]
        ).start()

        def dot(x, y):
            return jnp.sum(x * y, axis=0, keepdims=True)

        product_rz = dot(residual, precon)
        energy = DAMPING * dot(precon, precon)
        cross = jnp.zeros_like(product_rz) if turn == 0 else dot(precon, image)
        spread.wait()
        exchanges.append(spread)
        values = [None, None]
        for k in range(9):
            picked = pick([table[turn, n, k : k + 1] for n in range(blocks)], block_of, lane)
            for i in range(2):
                term = cam_rows[9 * i + k] * picked
                values[i] = term if k == 0 else values[i] + term
        point_terms(values)
        fresh = sum_into(staged(stage), point_hot[...])[:8]
        remain = remains(values, fresh)
        energy = energy + jnp.sum(values[0] * remain[0] + values[1] * remain[1], axis=0, keepdims=True)
        lanes_of = lax.broadcasted_iota(jnp.int32, (1, LANES), 1)
        product_rz, energy, cross = [
            jnp.sum(x, axis=1, keepdims=True) for x in (product_rz, energy, cross)
        ]
        sum_start(turn, jnp.where(lanes_of == 0, product_rz, jnp.where(lanes_of == 1, energy, cross)))
        last = turn + 1 == ITERS
        if not last:
            for k in range(9):
                put(stage, k, cam_rows[k] * remain[0] + cam_rows[9 + k] * remain[1])
            by_block(part.at[turn], sum_near(staged(stage), [mask[...] for mask in masks], cam_hot[...]))
            back = Near(
                2 + 2 * turn, lambda block: part.at[turn, block], lambda at: recv.at[turn, at]
            ).start()
            recv[turn, mine] = part[turn, mine]
        sum_middle(turn)
        following, energy, cross = sum_wait(turn)
        if turn == 0:
            curvature, direction, gathered = energy, precon, fresh
        else:
            ratio = following / current
            curvature = energy + ratio * (2.0 * cross + ratio * curvature)
            direction = precon + ratio * direction
            gathered = fresh + ratio * gathered
        current = following
        step_size = current / curvature
        cam_step = cam_step + step_size * direction
        point_total = point_total + step_size * gathered
        if not last:
            back.wait()
            exchanges.append(back)
            product = DAMPING * precon
            for n in range(blocks):
                product = product + recv[turn, n]
            image = product if turn == 0 else product + ratio * image
            residual = residual - step_size * image

    normal.finish()
    for exchange in exchanges:
        exchange.finish()
    for turn in range(ITERS):
        sum_finish(turn)
    cam_step_ref[...] = cam_step[:9]
    for j, row in enumerate(apply_three(inverse, rows_of(point_total, 3))):
        point_step_ref[j : j + 1, :] = -row


def local(groups, regions, cam_jacobian, point_jacobian, residuals, obs_camera, obs_point):
    count = obs_camera.shape[0]
    tiles = count // LANES
    blocks = 3 * groups
    inner = inner_regions(regions)
    phases = 2 * ITERS
    groups_wide = groups * C_DEV
    f32, bf16 = jnp.float32, jnp.bfloat16
    near = blocks - 1
    return pl.pallas_call(
        functools.partial(kernel, groups, regions),
        out_shape=(
            jax.ShapeDtypeStruct((9, C_DEV), f32),
            jax.ShapeDtypeStruct((3, P_DEV), f32),
        ),
        in_specs=[pl.BlockSpec(memory_space=pl.ANY)] * 5,
        out_specs=[pl.BlockSpec(memory_space=pltpu.VMEM)] * 2,
        scratch_shapes=[
            pltpu.VMEM(cam_jacobian.shape, bf16),
            pltpu.VMEM(point_jacobian.shape, bf16),
            pltpu.VMEM(residuals.shape, f32),
            pltpu.VMEM((tiles, LANES), jnp.int32),
            pltpu.VMEM((tiles, LANES), jnp.int32),
            pltpu.VMEM((18 * tiles, LANES), f32),
            pltpu.VMEM((6 * tiles, LANES), f32),
            pltpu.VMEM((2 * tiles, LANES), f32),
            pltpu.VMEM((count, groups_wide), bf16),
            pltpu.VMEM((count, P_DEV), bf16),
            pltpu.VMEM((tiles * ROWS, LANES), f32),
            pltpu.VMEM((3, ROWS, count), bf16),
            pltpu.VMEM((tiles * NORMAL_ROWS, LANES), f32),
            pltpu.VMEM((9, ROWS, C_DEV), f32),
            pltpu.VMEM((blocks, NORMAL_ROWS, C_DEV), f32),
            pltpu.VMEM((blocks, NORMAL_ROWS, C_DEV), f32),
            pltpu.VMEM((ITERS - 1, blocks, ROWS, C_DEV), f32),
            pltpu.VMEM((ITERS - 1, blocks, ROWS, C_DEV), f32),
            pltpu.VMEM((ITERS, blocks, ROWS, C_DEV), f32),
            pltpu.VMEM((ITERS, groups * inner, 1, LANES), f32),
            pltpu.VMEM((ITERS, regions // inner, 1, LANES), f32),
            pltpu.SemaphoreType.DMA((phases, near)),
            pltpu.SemaphoreType.DMA((phases, near)),
            pltpu.SemaphoreType.DMA((2, ITERS)),
            pltpu.SemaphoreType.DMA((2, ITERS)),
            pltpu.SemaphoreType.DMA((5,)),
        ],
        compiler_params=pltpu.CompilerParams(
            collective_id=0, has_side_effects=True, vmem_limit_bytes=48 * 1024 * 1024
        ),
    )(
        cam_jacobian,
        point_jacobian,
        residuals,
        obs_camera.reshape(tiles, LANES),
        obs_point.reshape(tiles, LANES),
    )


def solution(mesh):
    placed = (
        P(None, ("grp", "reg")),
        P(None, ("grp", "reg")),
        P(None, ("grp", "reg")),
        P(("grp", "reg")),
        P(("grp", "reg")),
    )
    return jax.shard_map(
        functools.partial(local, mesh.shape["grp"], mesh.shape["reg"]),
        mesh=mesh,
        in_specs=placed,
        out_specs=(P(None, ("grp", "reg")), P(None, ("grp", "reg"))),
        check_vma=False,
    )
```

```python
import functools

import jax
import jax.numpy as jnp
from jax import lax
from jax.experimental import pallas as pl
from jax.experimental.pallas import tpu as pltpu
from jax.sharding import PartitionSpec as P

C_DEV = 128
P_DEV = 256
ITERS = 3
DAMPING = 4.0

LANES = 128
ROWS = 16
PAIRS = [(i, j) for i in range(9) for j in range(i + 1)]
NORMAL_ROWS = 48
PARTS = 3
NORMAL_PARTS = 2
MESH = pl.DeviceIdType.MESH


def split(x, count):
    parts = []
    for _ in range(count - 1):
        part = x.astype(jnp.bfloat16).astype(jnp.float32)
        parts.append(part)
        x = x - part
    parts.append(x)
    return jnp.concatenate(parts, 0).astype(jnp.bfloat16)


def sum_parts(summed, count):
    rows = summed.shape[0] // count
    total = summed[(count - 1) * rows :]
    for part in range(count - 2, -1, -1):
        total = total + summed[part * rows : (part + 1) * rows]
    return total


def sum_into(terms, onehot, count=PARTS):
    summed = jnp.dot(split(terms, count), onehot, preferred_element_type=jnp.float32)
    return sum_parts(summed, count)


def sum_near(terms, masks, onehot, count=PARTS):
    parts = split(terms, count)
    masked = []
    for mask in masks:
        masked.append(parts * jnp.concatenate([mask] * (parts.shape[0] // mask.shape[0]), 0))
    summed = jnp.dot(jnp.concatenate(masked, 0), onehot, preferred_element_type=jnp.float32)
    rows = parts.shape[0]
    return [sum_parts(summed[n * rows : (n + 1) * rows], count) for n in range(len(masks))]


def inverse_three(a, b, c, e, f, i):
    adjoint = [e * i - f * f, c * f - b * i, b * f - c * e, a * i - c * c, b * c - a * f, a * e - b * b]
    determinant = a * adjoint[0] + b * adjoint[1] + c * adjoint[2]
    return [entry / determinant for entry in adjoint]


def apply_three(inverse, vector):
    a, b, c, e, f, i = inverse
    x, y, z = vector
    return [a * x + b * y + c * z, b * x + e * y + f * z, c * x + f * y + i * z]


def block_inverse(entry):
    work = {(i, j): entry(i, j) for i, j in PAIRS}
    for p in range(9):
        scale = 1.0 / work[p, p]
        column = [work[max(i, p), min(i, p)] for i in range(9)]
        scaled = [value * scale for value in column]
        for i, j in PAIRS:
            if i == p and j == p:
                work[i, j] = -scale
            elif i == p:
                work[i, j] = scaled[j]
            elif j == p:
                work[i, j] = scaled[i]
            else:
                work[i, j] = work[i, j] - column[i] * scaled[j]
    return work


def inner_regions(regions):
    return max(n for n in range(1, regions + 1) if regions % n == 0 and n * n <= regions)


def kernel(
    groups,
    regions,
    cam_in,
    point_in,
    res_in,
    camera_in,
    slot_in,
    cam_step_ref,
    point_step_ref,
    cam_ref,
    point_ref,
    res_ref,
    camera_ref,
    slot_ref,
    cam_store,
    point_store,
    res_store,
    cam_hot,
    point_hot,
    stage,
    near_mask,
    normal_stage,
    solve,
    normal_part,
    normal_recv,
    part,
    recv,
    table,
    first_sums,
    second_sums,
    near_send,
    near_recv,
    sum_send,
    sum_recv,
    load,
):
    group = lax.axis_index("grp")
    region = lax.axis_index("reg")
    blocks = 3 * groups
    tiles = camera_ref.shape[0]

    loads = [
        pltpu.make_async_copy(source, target, load.at[n])
        for n, (source, target) in enumerate(
            [
                (camera_in, camera_ref),
                (slot_in, slot_ref),
                (cam_in, cam_ref),
                (point_in, point_ref),
                (res_in, res_ref),
            ]
        )
    ]
    for copy in loads:
        copy.start()

    def turned(position, step, size):
        return lax.select(position + step >= size, position + step - size, position + step)

    inner = inner_regions(regions)
    outer = regions // inner
    within = lax.rem(region, inner)
    plane = region // inner
    others_group = [turned(group, j, groups) for j in range(groups)]
    others_within = [turned(within, j, inner) for j in range(inner)]
    others_plane = [turned(plane, j, outer) for j in range(outer)]
    first_level = [(g, plane * inner + r) for r in others_within for g in others_group][1:]
    second_level = [(group, p * inner + within) for p in others_plane][1:]
    first_me = group * inner + within
    beside = [(g, turned(region, step, regions)) for step in (1, regions - 1) for g in others_group]

    barrier = pltpu.get_barrier_semaphore()
    for other in first_level + second_level + beside:
        pl.semaphore_signal(barrier, inc=1, device_id=other, device_id_type=MESH)
    greeted = len(first_level) + len(second_level) + len(beside)

    mine = groups + group
    has_below, has_above = region > 0, region < regions - 1

    class Near:
        def __init__(self, phase, source, target):
            self.copies = [[], [], []]
            n = 0
            for offset in range(3):
                for j in range(1 if offset == 1 else 0, groups):
                    other = others_group[j]
                    self.copies[offset].append(
                        pltpu.make_async_remote_copy(
                            src_ref=source(offset * groups + other),
                            dst_ref=target((2 - offset) * groups + group),
                            send_sem=near_send.at[phase, n],
                            recv_sem=near_recv.at[phase, n],
                            device_id=(other, turned(region, (offset - 1) % regions, regions)),
                            device_id_type=MESH,
                        )
                    )
                    n += 1

        def each(self, below, above, act):
            @pl.when(has_below)
            def _():
                for copy in self.copies[below]:
                    act(copy)

            @pl.when(has_above)
            def _():
                for copy in self.copies[above]:
                    act(copy)

            for copy in self.copies[1]:
                act(copy)

        def start(self):
            self.each(0, 2, lambda copy: copy.start())
            return self

        def wait(self):
            self.each(2, 0, lambda copy: copy.wait_recv())

        def finish(self):
            self.each(0, 2, lambda copy: copy.wait_send())

    def clear_ends(ref):
        @pl.when(region == 0)
        def _():
            for j in range(groups):
                ref[j] = jnp.zeros(ref.shape[1:], jnp.float32)

        @pl.when(region == regions - 1)
        def _():
            for j in range(groups):
                ref[2 * groups + j] = jnp.zeros(ref.shape[1:], jnp.float32)

    def push(ref, at, others, level, phase):
        for other in others:
            pltpu.make_async_remote_copy(
                src_ref=ref.at[phase, at],
                dst_ref=ref.at[phase, at],
                send_sem=sum_send.at[level, phase],
                recv_sem=sum_recv.at[level, phase],
                device_id=other,
                device_id_type=MESH,
            ).start()

    def pulled(ref, count, level, phase):
        bytes_of = ref.at[phase, pl.ds(0, count)]
        pltpu.make_async_copy(bytes_of, bytes_of, sum_recv.at[level, phase]).wait()
        return jnp.sum(ref[phase], axis=0)

    def sum_start(phase, row):
        first_sums[phase, first_me] = row
        push(first_sums, first_me, first_level, 0, phase)

    def sum_middle(phase):
        second_sums[phase, plane] = pulled(first_sums, len(first_level), 0, phase)
        push(second_sums, plane, second_level, 1, phase)

    def sum_wait(phase):
        sums = pulled(second_sums, len(second_level), 1, phase)
        return [sums[:, n : n + 1] for n in range(3)]

    def sum_finish(phase):
        for level, (ref, others) in enumerate([(first_sums, first_level), (second_sums, second_level)]):
            bytes_of = ref.at[phase, pl.ds(0, len(others))]
            pltpu.make_async_copy(bytes_of, bytes_of, sum_send.at[level, phase]).wait()

    clear_ends(normal_recv)
    for turn in range(ITERS):
        clear_ends(table.at[turn])
        clear_ends(recv.at[turn])
    stage[...] = jnp.zeros_like(stage)
    normal_stage[...] = jnp.zeros_like(normal_stage)

    for copy in loads[:2]:
        copy.wait()
    camera = camera_ref[...]
    owner = jnp.right_shift(camera, C_DEV.bit_length() - 1)
    lane = jnp.bitwise_and(camera, C_DEV - 1)
    owner_group = jnp.zeros_like(owner)
    for j in range(1, groups):
        owner_group = owner_group + jnp.where(owner >= j * regions, 1, 0)
    offset_of = owner - owner_group * regions - region + 1
    block_of = offset_of * groups + owner_group
    for n in range(3):
        here = jnp.where(offset_of == n, 1.0, 0.0)
        for s in range(tiles):
            row = jnp.broadcast_to(here[s : s + 1], (ROWS, LANES))
            near_mask[n, :, s * LANES : (s + 1) * LANES] = row.astype(jnp.bfloat16)
    slot = slot_ref[...]
    point_lane = jnp.bitwise_and(slot, LANES - 1)
    point_tile = jnp.right_shift(slot, LANES.bit_length() - 1)

    column_t = jnp.transpose((owner_group * C_DEV + lane).astype(jnp.float32))
    cam_iota = lax.broadcasted_iota(jnp.int32, (LANES, groups * C_DEV), 1).astype(jnp.float32)
    for s in range(tiles):
        at = slice(s * LANES, (s + 1) * LANES)
        cam_hot[at, :] = jnp.where(column_t[:, s : s + 1] == cam_iota, 1.0, 0.0).astype(jnp.bfloat16)

    for copy in loads[2:]:
        copy.wait()
    for s in range(tiles):
        lanes = slice(s * LANES, (s + 1) * LANES)
        cam_store[pl.ds(s, 18, stride=tiles), :] = cam_ref[:, lanes].astype(jnp.float32)
        point_store[pl.ds(s, 6, stride=tiles), :] = point_ref[:, lanes].astype(jnp.float32)
        res_store[pl.ds(s, 2, stride=tiles), :] = res_ref[:, lanes]
    cam_rows = [cam_store[n * tiles : (n + 1) * tiles] for n in range(18)]
    point_rows = [point_store[n * tiles : (n + 1) * tiles] for n in range(6)]
    residuals = [res_store[n * tiles : (n + 1) * tiles] for n in range(2)]

    def put(ref, row, term):
        ref[pl.ds(row, tiles, stride=ref.shape[0] // tiles), :] = term

    def staged(ref):
        rows = ref.shape[0] // tiles
        return jnp.concatenate([ref[s * rows : (s + 1) * rows] for s in range(tiles)], 1)

    def pick(rows, tile, at):
        total = None
        for n, row in enumerate(rows):
            wide = jnp.broadcast_to(row, (tiles, LANES))
            got = jnp.take_along_axis(wide, at, axis=1, mode="promise_in_bounds")
            total = got if total is None else jnp.where(tile == n, got, total)
        return total

    def point_terms(values):
        for j in range(3):
            put(stage, j, point_rows[j] * values[0] + point_rows[3 + j] * values[1])

    masks = [near_mask.at[n] for n in range(3)]

    def by_block(ref, summed):
        for n in range(3):
            for j in range(groups):
                ref[n * groups + j] = summed[n][:, j * C_DEV : (j + 1) * C_DEV]

    def rows_of(block, count):
        return [block[j : j + 1] for j in range(count)]

    def remains(values, gathered):
        solved = apply_three(inverse, rows_of(gathered, 3))
        picked = [
            pick([row[:, n * LANES : (n + 1) * LANES] for n in range(P_DEV // LANES)], point_tile, point_lane)
            for row in solved
        ]
        return [
            values[i]
            - (
                point_rows[3 * i] * picked[0]
                + point_rows[3 * i + 1] * picked[1]
                + point_rows[3 * i + 2] * picked[2]
            )
            for i in range(2)
        ]

    for n, (i, j) in enumerate(PAIRS):
        put(normal_stage, n, cam_rows[i] * cam_rows[j] + cam_rows[9 + i] * cam_rows[9 + j])
    by_block(
        normal_part,
        sum_near(staged(normal_stage), [mask[...] for mask in masks], cam_hot[...], NORMAL_PARTS),
    )
    pl.semaphore_wait(barrier, greeted)
    normal = Near(0, lambda block: normal_part.at[block], lambda at: normal_recv.at[at]).start()
    normal_recv[mine] = normal_part[mine]

    slot_t = jnp.transpose(slot.astype(jnp.float32))
    point_iota = lax.broadcasted_iota(jnp.int32, (LANES, P_DEV), 1).astype(jnp.float32)
    for s in range(tiles):
        at = slice(s * LANES, (s + 1) * LANES)
        point_hot[at, :] = jnp.where(slot_t[:, s : s + 1] == point_iota, 1.0, 0.0).astype(jnp.bfloat16)
    first = [residuals[0], residuals[1]]
    point_terms(first)
    for n, (i, j) in enumerate([(0, 0), (0, 1), (0, 2), (1, 1), (1, 2), (2, 2)]):
        put(stage, 3 + n, point_rows[i] * point_rows[j] + point_rows[3 + i] * point_rows[3 + j])
    sums = sum_into(staged(stage), point_hot[...])
    entries = rows_of(sums[3:9], 6)
    for n in (0, 3, 5):
        entries[n] = entries[n] + DAMPING
    inverse = inverse_three(*entries)
    point_total = sums[:8]

    def send_back(phase, at, remain):
        for k in range(9):
            put(stage, k, cam_rows[k] * remain[0] + cam_rows[9 + k] * remain[1])
        by_block(part.at[at], sum_near(staged(stage), [mask[...] for mask in masks], cam_hot[...]))
        back = Near(
            phase, lambda block: part.at[at, block, pl.ds(0, 9)], lambda block: recv.at[at, block]
        ).start()
        recv[at, mine] = part[at, mine, :9]
        return back

    def taken_back(at):
        out = recv[at, 0]
        for n in range(1, blocks):
            out = out + recv[at, n]
        return out

    gradient = send_back(1, ITERS - 1, remains(first, sums))
    normal.wait()
    total = normal_recv[0]
    for n in range(1, blocks):
        total = total + normal_recv[n]

    def entry(i, j):
        n = PAIRS.index((i, j))
        row = total[n : n + 1]
        return row + DAMPING if i == j else row

    minus_inverse = block_inverse(entry)
    for i, j in PAIRS:
        solve[i, j : j + 1, :] = -minus_inverse[i, j]
        if i != j:
            solve[j, i : i + 1, :] = -minus_inverse[i, j]

    def precondition(field):
        out = solve[0] * field[0:1]
        for k in range(1, 9):
            out = out + solve[k] * field[k : k + 1]
        return out

    def dot(x, y):
        return jnp.sum(x * y, axis=0, keepdims=True)

    def moved(x, scale, y):
        return [a + scale * b for a, b in zip(x, y)]

    gradient.wait()
    exchanges = [normal, gradient]
    lanes_of = lax.broadcasted_iota(jnp.int32, (1, LANES), 1)
    residual = -taken_back(ITERS - 1)
    field = precondition(residual)
    cam_step = jnp.zeros((9, C_DEV), jnp.float32)
    z = direction = slope = image = product = current = curvature = None
    for turn in range(ITERS):
        table[turn, mine] = field
        spread = Near(
            2 + 2 * turn, lambda block: table.at[turn, mine], lambda at: table.at[turn, at]
        ).start()
        exchanges.append(spread)
        spread.wait()
        if turn > 0:
            following, energy, cross = sum_wait(turn - 1)
        values = [None, None]
        for k in range(9):
            picked = pick([table[turn, n, k : k + 1] for n in range(blocks)], block_of, lane)
            for i in range(2):
                term = cam_rows[9 * i + k] * picked
                values[i] = term if k == 0 else values[i] + term
        point_terms(values)
        fresh = [field] + values + [sum_into(staged(stage), point_hot[...])[:8]]
        if turn == 0:
            z = fresh
        else:
            if turn == 1:
                curvature, direction, slope, image = energy, [z[0], z[3]], fresh, product
            else:
                ratio = following / current
                curvature = energy + ratio * (2.0 * cross + ratio * curvature)
                direction = moved([z[0], z[3]], ratio, direction)
                slope = moved(fresh, ratio, slope)
                image = product + ratio * image
            current = following
            step_size = current / curvature
            cam_step = cam_step + step_size * direction[0]
            point_total = point_total + step_size * direction[1]
            residual = residual - step_size * image
            z = moved(z, -step_size, slope)
        remain = remains(z[1:3], z[3])
        sums_of = [
            dot(residual, z[0]),
            DAMPING * dot(z[0], z[0]) + dot(z[1], remain[0]) + dot(z[2], remain[1]),
            jnp.zeros((1, LANES), jnp.float32) if turn == 0 else dot(z[0], image),
        ]
        sums_of = [jnp.sum(x, axis=1, keepdims=True) for x in sums_of]
        sum_start(turn, jnp.where(lanes_of == 0, sums_of[0], jnp.where(lanes_of == 1, sums_of[1], sums_of[2])))
        if turn + 1 < ITERS:
            back = send_back(3 + 2 * turn, turn, remain)
            exchanges.append(back)
            back.wait()
            sum_middle(turn)
            product = DAMPING * z[0] + taken_back(turn)
            field = precondition(product)

    sum_middle(ITERS - 1)
    following, energy, cross = sum_wait(ITERS - 1)
    ratio = following / current
    curvature = energy + ratio * (2.0 * cross + ratio * curvature)
    direction = moved([z[0], z[3]], ratio, direction)
    step_size = following / curvature
    cam_step = cam_step + step_size * direction[0]
    point_total = point_total + step_size * direction[1]
    for exchange in exchanges:
        exchange.finish()
    for turn in range(ITERS):
        sum_finish(turn)
    cam_step_ref[...] = cam_step
    for j, row in enumerate(apply_three(inverse, rows_of(point_total, 3))):
        point_step_ref[j : j + 1, :] = -row


def local(groups, regions, cam_jacobian, point_jacobian, residuals, obs_camera, obs_point):
    count = obs_camera.shape[0]
    tiles = count // LANES
    blocks = 3 * groups
    inner = inner_regions(regions)
    phases = 2 * ITERS + 1
    groups_wide = groups * C_DEV
    f32, bf16 = jnp.float32, jnp.bfloat16
    near = blocks - 1
    return pl.pallas_call(
        functools.partial(kernel, groups, regions),
        out_shape=(
            jax.ShapeDtypeStruct((9, C_DEV), f32),
            jax.ShapeDtypeStruct((3, P_DEV), f32),
        ),
        in_specs=[pl.BlockSpec(memory_space=pl.ANY)] * 5,
        out_specs=[pl.BlockSpec(memory_space=pltpu.VMEM)] * 2,
        scratch_shapes=[
            pltpu.VMEM(cam_jacobian.shape, bf16),
            pltpu.VMEM(point_jacobian.shape, bf16),
            pltpu.VMEM(residuals.shape, f32),
            pltpu.VMEM((tiles, LANES), jnp.int32),
            pltpu.VMEM((tiles, LANES), jnp.int32),
            pltpu.VMEM((18 * tiles, LANES), f32),
            pltpu.VMEM((6 * tiles, LANES), f32),
            pltpu.VMEM((2 * tiles, LANES), f32),
            pltpu.VMEM((count, groups_wide), bf16),
            pltpu.VMEM((count, P_DEV), bf16),
            pltpu.VMEM((tiles * ROWS, LANES), f32),
            pltpu.VMEM((3, ROWS, count), bf16),
            pltpu.VMEM((tiles * NORMAL_ROWS, LANES), f32),
            pltpu.VMEM((9, 9, C_DEV), f32),
            pltpu.VMEM((blocks, NORMAL_ROWS, C_DEV), f32),
            pltpu.VMEM((blocks, NORMAL_ROWS, C_DEV), f32),
            pltpu.VMEM((ITERS, blocks, ROWS, C_DEV), f32),
            pltpu.VMEM((ITERS, blocks, 9, C_DEV), f32),
            pltpu.VMEM((ITERS, blocks, 9, C_DEV), f32),
            pltpu.VMEM((ITERS, groups * inner, 1, LANES), f32),
            pltpu.VMEM((ITERS, regions // inner, 1, LANES), f32),
            pltpu.SemaphoreType.DMA((phases, near)),
            pltpu.SemaphoreType.DMA((phases, near)),
            pltpu.SemaphoreType.DMA((2, ITERS)),
            pltpu.SemaphoreType.DMA((2, ITERS)),
            pltpu.SemaphoreType.DMA((5,)),
        ],
        compiler_params=pltpu.CompilerParams(
            collective_id=0, has_side_effects=True, vmem_limit_bytes=48 * 1024 * 1024
        ),
    )(
        cam_jacobian,
        point_jacobian,
        residuals,
        obs_camera.reshape(tiles, LANES),
        obs_point.reshape(tiles, LANES),
    )


def solution(mesh):
    placed = (
        P(None, ("grp", "reg")),
        P(None, ("grp", "reg")),
        P(None, ("grp", "reg")),
        P(("grp", "reg")),
        P(("grp", "reg")),
    )
    return jax.shard_map(
        functools.partial(local, mesh.shape["grp"], mesh.shape["reg"]),
        mesh=mesh,
        in_specs=placed,
        out_specs=(P(None, ("grp", "reg")), P(None, ("grp", "reg"))),
        check_vma=False,
    )
```

```python
import functools

import jax
import jax.numpy as jnp
from jax import lax
from jax.experimental import pallas as pl
from jax.experimental.pallas import tpu as pltpu
from jax.sharding import PartitionSpec as P

C_DEV = 128
P_DEV = 256
ITERS = 3
DAMPING = 4.0

LANES = 128
ROWS = 16
PAIRS = [(i, j) for i in range(9) for j in range(i + 1)]
NORMAL_ROWS = 48
PARTS = 3
CAMERA_PARTS = 2
HALVES = 2
MESH = pl.DeviceIdType.MESH


def split(x, count):
    parts = []
    for _ in range(count - 1):
        part = x.astype(jnp.bfloat16).astype(jnp.float32)
        parts.append(part)
        x = x - part
    parts.append(x)
    return jnp.concatenate(parts, 0).astype(jnp.bfloat16)


def product(left, onehot):
    run = onehot.shape[0] // HALVES
    total = None
    for n in range(HALVES):
        at = slice(n * run, (n + 1) * run)
        part = jnp.dot(left[:, at], onehot[at], preferred_element_type=jnp.float32)
        total = part if total is None else total + part
    return total


def sum_parts(summed, count):
    rows = summed.shape[0] // count
    total = summed[(count - 1) * rows :]
    for part in range(count - 2, -1, -1):
        total = total + summed[part * rows : (part + 1) * rows]
    return total


def sum_into(terms, onehot, count=PARTS):
    return sum_parts(product(split(terms, count), onehot), count)


def sum_near(terms, masks, onehot, count=CAMERA_PARTS):
    parts = split(terms, count)
    masked = []
    for mask in masks:
        masked.append(parts * jnp.concatenate([mask] * (parts.shape[0] // mask.shape[0]), 0))
    summed = product(jnp.concatenate(masked, 0), onehot)
    rows = parts.shape[0]
    return [sum_parts(summed[n * rows : (n + 1) * rows], count) for n in range(len(masks))]


def inverse_three(a, b, c, e, f, i):
    adjoint = [e * i - f * f, c * f - b * i, b * f - c * e, a * i - c * c, b * c - a * f, a * e - b * b]
    determinant = a * adjoint[0] + b * adjoint[1] + c * adjoint[2]
    return [entry / determinant for entry in adjoint]


def apply_three(inverse, vector):
    a, b, c, e, f, i = inverse
    x, y, z = vector
    return [a * x + b * y + c * z, b * x + e * y + f * z, c * x + f * y + i * z]


def block_inverse(entry):
    work = {(i, j): entry(i, j) for i, j in PAIRS}
    for p in range(9):
        scale = 1.0 / work[p, p]
        column = [work[max(i, p), min(i, p)] for i in range(9)]
        scaled = [value * scale for value in column]
        for i, j in PAIRS:
            if i == p and j == p:
                work[i, j] = -scale
            elif i == p:
                work[i, j] = scaled[j]
            elif j == p:
                work[i, j] = scaled[i]
            else:
                work[i, j] = work[i, j] - column[i] * scaled[j]
    return work


def inner_regions(regions):
    return max(n for n in range(1, regions + 1) if regions % n == 0 and n * n <= regions)


def kernel(
    groups,
    regions,
    cam_in,
    point_in,
    res_in,
    camera_in,
    slot_in,
    cam_step_ref,
    point_step_ref,
    cam_ref,
    point_ref,
    res_ref,
    camera_ref,
    slot_ref,
    cam_store,
    point_store,
    res_store,
    cam_hot,
    point_hot,
    stage,
    near_mask,
    normal_stage,
    solve,
    normal_part,
    normal_recv,
    part,
    recv,
    table,
    first_sums,
    second_sums,
    near_send,
    near_recv,
    sum_send,
    sum_recv,
    load,
):
    group = lax.axis_index("grp")
    region = lax.axis_index("reg")
    blocks = 3 * groups
    tiles = camera_ref.shape[0]

    loads = [
        pltpu.make_async_copy(source, target, load.at[n])
        for n, (source, target) in enumerate(
            [
                (camera_in, camera_ref),
                (slot_in, slot_ref),
                (cam_in, cam_ref),
                (point_in, point_ref),
                (res_in, res_ref),
            ]
        )
    ]
    for copy in loads:
        copy.start()

    def turned(position, step, size):
        return lax.select(position + step >= size, position + step - size, position + step)

    inner = inner_regions(regions)
    outer = regions // inner
    within = lax.rem(region, inner)
    plane = region // inner
    others_group = [turned(group, j, groups) for j in range(groups)]
    others_within = [turned(within, j, inner) for j in range(inner)]
    others_plane = [turned(plane, j, outer) for j in range(outer)]
    first_level = [(g, plane * inner + r) for r in others_within for g in others_group][1:]
    second_level = [(group, p * inner + within) for p in others_plane][1:]
    first_me = group * inner + within
    beside = [(g, turned(region, step, regions)) for step in (1, regions - 1) for g in others_group]

    barrier = pltpu.get_barrier_semaphore()
    for other in first_level + second_level + beside:
        pl.semaphore_signal(barrier, inc=1, device_id=other, device_id_type=MESH)
    greeted = len(first_level) + len(second_level) + len(beside)

    mine = groups + group
    has_below, has_above = region > 0, region < regions - 1

    class Near:
        def __init__(self, phase, source, target):
            self.copies = [[], [], []]
            n = 0
            for offset in range(3):
                for j in range(1 if offset == 1 else 0, groups):
                    other = others_group[j]
                    self.copies[offset].append(
                        pltpu.make_async_remote_copy(
                            src_ref=source(offset * groups + other),
                            dst_ref=target((2 - offset) * groups + group),
                            send_sem=near_send.at[phase, n],
                            recv_sem=near_recv.at[phase, n],
                            device_id=(other, turned(region, (offset - 1) % regions, regions)),
                            device_id_type=MESH,
                        )
                    )
                    n += 1

        def each(self, below, above, act):
            @pl.when(has_below)
            def _():
                for copy in self.copies[below]:
                    act(copy)

            @pl.when(has_above)
            def _():
                for copy in self.copies[above]:
                    act(copy)

            for copy in self.copies[1]:
                act(copy)

        def start(self):
            self.each(0, 2, lambda copy: copy.start())
            return self

        def wait(self):
            self.each(2, 0, lambda copy: copy.wait_recv())

        def finish(self):
            self.each(0, 2, lambda copy: copy.wait_send())

    def clear_ends(ref):
        @pl.when(region == 0)
        def _():
            for j in range(groups):
                ref[j] = jnp.zeros(ref.shape[1:], jnp.float32)

        @pl.when(region == regions - 1)
        def _():
            for j in range(groups):
                ref[2 * groups + j] = jnp.zeros(ref.shape[1:], jnp.float32)

    def push(ref, at, others, level, phase):
        for other in others:
            pltpu.make_async_remote_copy(
                src_ref=ref.at[phase, at],
                dst_ref=ref.at[phase, at],
                send_sem=sum_send.at[level, phase],
                recv_sem=sum_recv.at[level, phase],
                device_id=other,
                device_id_type=MESH,
            ).start()

    def pulled(ref, count, level, phase):
        bytes_of = ref.at[phase, pl.ds(0, count)]
        pltpu.make_async_copy(bytes_of, bytes_of, sum_recv.at[level, phase]).wait()
        return jnp.sum(ref[phase], axis=0)

    def sum_start(phase, row):
        first_sums[phase, first_me] = row
        push(first_sums, first_me, first_level, 0, phase)

    def sum_middle(phase):
        second_sums[phase, plane] = pulled(first_sums, len(first_level), 0, phase)
        push(second_sums, plane, second_level, 1, phase)

    def sum_wait(phase):
        sums = pulled(second_sums, len(second_level), 1, phase)
        return [sums[:, n : n + 1] for n in range(3)]

    def sum_finish(phase):
        for level, (ref, others) in enumerate([(first_sums, first_level), (second_sums, second_level)]):
            bytes_of = ref.at[phase, pl.ds(0, len(others))]
            pltpu.make_async_copy(bytes_of, bytes_of, sum_send.at[level, phase]).wait()

    clear_ends(normal_recv)
    for turn in range(ITERS):
        clear_ends(table.at[turn])
        clear_ends(recv.at[turn])
    stage[...] = jnp.zeros_like(stage)
    normal_stage[...] = jnp.zeros_like(normal_stage)

    for copy in loads[:2]:
        copy.wait()
    camera = camera_ref[...]
    owner = jnp.right_shift(camera, C_DEV.bit_length() - 1)
    lane = jnp.bitwise_and(camera, C_DEV - 1)
    owner_group = jnp.zeros_like(owner)
    for j in range(1, groups):
        owner_group = owner_group + jnp.where(owner >= j * regions, 1, 0)
    offset_of = owner - owner_group * regions - region + 1
    block_of = offset_of * groups + owner_group
    for n in range(3):
        here = jnp.where(offset_of == n, 1.0, 0.0)
        for s in range(tiles):
            row = jnp.broadcast_to(here[s : s + 1], (ROWS, LANES))
            near_mask[n, :, s * LANES : (s + 1) * LANES] = row.astype(jnp.bfloat16)
    slot = slot_ref[...]
    point_lane = jnp.bitwise_and(slot, LANES - 1)
    point_tile = jnp.right_shift(slot, LANES.bit_length() - 1)

    column_t = jnp.transpose((owner_group * C_DEV + lane).astype(jnp.float32))
    cam_iota = lax.broadcasted_iota(jnp.int32, (LANES, groups * C_DEV), 1).astype(jnp.float32)
    for s in range(tiles):
        at = slice(s * LANES, (s + 1) * LANES)
        cam_hot[at, :] = jnp.where(column_t[:, s : s + 1] == cam_iota, 1.0, 0.0).astype(jnp.bfloat16)

    for copy in loads[2:]:
        copy.wait()
    for s in range(tiles):
        lanes = slice(s * LANES, (s + 1) * LANES)
        cam_store[pl.ds(s, 18, stride=tiles), :] = cam_ref[:, lanes].astype(jnp.float32)
        point_store[pl.ds(s, 6, stride=tiles), :] = point_ref[:, lanes].astype(jnp.float32)
        res_store[pl.ds(s, 2, stride=tiles), :] = res_ref[:, lanes]
    cam_rows = [cam_store[n * tiles : (n + 1) * tiles] for n in range(18)]
    point_rows = [point_store[n * tiles : (n + 1) * tiles] for n in range(6)]
    residuals = [res_store[n * tiles : (n + 1) * tiles] for n in range(2)]

    def put(ref, row, term):
        ref[pl.ds(row, tiles, stride=ref.shape[0] // tiles), :] = term

    def staged(ref):
        rows = ref.shape[0] // tiles
        return jnp.concatenate([ref[s * rows : (s + 1) * rows] for s in range(tiles)], 1)

    def pick(rows, tile, at):
        total = None
        for n, row in enumerate(rows):
            wide = jnp.broadcast_to(row, (tiles, LANES))
            got = jnp.take_along_axis(wide, at, axis=1, mode="promise_in_bounds")
            total = got if total is None else jnp.where(tile == n, got, total)
        return total

    def point_terms(values):
        for j in range(3):
            put(stage, j, point_rows[j] * values[0] + point_rows[3 + j] * values[1])

    masks = [near_mask.at[n] for n in range(3)]

    def by_block(ref, summed):
        for n in range(3):
            for j in range(groups):
                ref[n * groups + j] = summed[n][:, j * C_DEV : (j + 1) * C_DEV]

    def rows_of(block, count):
        return [block[j : j + 1] for j in range(count)]

    def remains(values, gathered):
        solved = apply_three(inverse, rows_of(gathered, 3))
        picked = [
            pick([row[:, n * LANES : (n + 1) * LANES] for n in range(P_DEV // LANES)], point_tile, point_lane)
            for row in solved
        ]
        return [
            values[i]
            - (
                point_rows[3 * i] * picked[0]
                + point_rows[3 * i + 1] * picked[1]
                + point_rows[3 * i + 2] * picked[2]
            )
            for i in range(2)
        ]

    for n, (i, j) in enumerate(PAIRS):
        put(normal_stage, n, cam_rows[i] * cam_rows[j] + cam_rows[9 + i] * cam_rows[9 + j])
    by_block(
        normal_part,
        sum_near(staged(normal_stage), [mask[...] for mask in masks], cam_hot[...]),
    )
    pl.semaphore_wait(barrier, greeted)
    normal = Near(0, lambda block: normal_part.at[block], lambda at: normal_recv.at[at]).start()
    normal_recv[mine] = normal_part[mine]

    slot_t = jnp.transpose(slot.astype(jnp.float32))
    point_iota = lax.broadcasted_iota(jnp.int32, (LANES, P_DEV), 1).astype(jnp.float32)
    for s in range(tiles):
        at = slice(s * LANES, (s + 1) * LANES)
        point_hot[at, :] = jnp.where(slot_t[:, s : s + 1] == point_iota, 1.0, 0.0).astype(jnp.bfloat16)
    first = [residuals[0], residuals[1]]
    point_terms(first)
    for n, (i, j) in enumerate([(0, 0), (0, 1), (0, 2), (1, 1), (1, 2), (2, 2)]):
        put(stage, 3 + n, point_rows[i] * point_rows[j] + point_rows[3 + i] * point_rows[3 + j])
    sums = sum_into(staged(stage), point_hot[...])
    entries = rows_of(sums[3:9], 6)
    for n in (0, 3, 5):
        entries[n] = entries[n] + DAMPING
    inverse = inverse_three(*entries)
    point_total = sums[:8]

    def send_back(phase, at, remain):
        for k in range(9):
            put(stage, k, cam_rows[k] * remain[0] + cam_rows[9 + k] * remain[1])
        by_block(part.at[at], sum_near(staged(stage), [mask[...] for mask in masks], cam_hot[...]))
        back = Near(
            phase, lambda block: part.at[at, block, pl.ds(0, 9)], lambda block: recv.at[at, block]
        ).start()
        recv[at, mine] = part[at, mine, :9]
        return back

    def taken_back(at):
        out = recv[at, 0]
        for n in range(1, blocks):
            out = out + recv[at, n]
        return out

    gradient = send_back(1, ITERS - 1, remains(first, sums))
    normal.wait()
    total = normal_recv[0]
    for n in range(1, blocks):
        total = total + normal_recv[n]

    def entry(i, j):
        n = PAIRS.index((i, j))
        row = total[n : n + 1]
        return row + DAMPING if i == j else row

    minus_inverse = block_inverse(entry)
    for i, j in PAIRS:
        solve[i, j : j + 1, :] = -minus_inverse[i, j]
        if i != j:
            solve[j, i : i + 1, :] = -minus_inverse[i, j]

    def precondition(field):
        out = solve[0] * field[0:1]
        for k in range(1, 9):
            out = out + solve[k] * field[k : k + 1]
        return out

    def dot(x, y):
        return jnp.sum(x * y, axis=0, keepdims=True)

    def moved(x, scale, y):
        return [a + scale * b for a, b in zip(x, y)]

    gradient.wait()
    exchanges = [normal, gradient]
    lanes_of = lax.broadcasted_iota(jnp.int32, (1, LANES), 1)
    residual = -taken_back(ITERS - 1)
    field = precondition(residual)
    cam_step = jnp.zeros((9, C_DEV), jnp.float32)
    z = direction = slope = image = product = current = curvature = None
    for turn in range(ITERS):
        table[turn, mine] = field
        spread = Near(
            2 + 2 * turn, lambda block: table.at[turn, mine], lambda at: table.at[turn, at]
        ).start()
        exchanges.append(spread)
        spread.wait()
        if turn > 0:
            following, energy, cross = sum_wait(turn - 1)
        values = [None, None]
        for k in range(9):
            picked = pick([table[turn, n, k : k + 1] for n in range(blocks)], block_of, lane)
            for i in range(2):
                term = cam_rows[9 * i + k] * picked
                values[i] = term if k == 0 else values[i] + term
        point_terms(values)
        fresh = [field] + values + [sum_into(staged(stage), point_hot[...])[:8]]
        if turn == 0:
            z = fresh
        else:
            if turn == 1:
                curvature, direction, slope, image = energy, [z[0], z[3]], fresh, product
            else:
                ratio = following / current
                curvature = energy + ratio * (2.0 * cross + ratio * curvature)
                direction = moved([z[0], z[3]], ratio, direction)
                slope = moved(fresh, ratio, slope)
                image = product + ratio * image
            current = following
            step_size = current / curvature
            cam_step = cam_step + step_size * direction[0]
            point_total = point_total + step_size * direction[1]
            residual = residual - step_size * image
            z = moved(z, -step_size, slope)
        remain = remains(z[1:3], z[3])
        sums_of = [
            dot(residual, z[0]),
            DAMPING * dot(z[0], z[0]) + dot(z[1], remain[0]) + dot(z[2], remain[1]),
            jnp.zeros((1, LANES), jnp.float32) if turn == 0 else dot(z[0], image),
        ]
        sums_of = [jnp.sum(x, axis=1, keepdims=True) for x in sums_of]
        sum_start(turn, jnp.where(lanes_of == 0, sums_of[0], jnp.where(lanes_of == 1, sums_of[1], sums_of[2])))
        if turn + 1 < ITERS:
            back = send_back(3 + 2 * turn, turn, remain)
            exchanges.append(back)
            back.wait()
            sum_middle(turn)
            product = DAMPING * z[0] + taken_back(turn)
            field = precondition(product)

    sum_middle(ITERS - 1)
    following, energy, cross = sum_wait(ITERS - 1)
    ratio = following / current
    curvature = energy + ratio * (2.0 * cross + ratio * curvature)
    direction = moved([z[0], z[3]], ratio, direction)
    step_size = following / curvature
    cam_step = cam_step + step_size * direction[0]
    point_total = point_total + step_size * direction[1]
    for exchange in exchanges:
        exchange.finish()
    for turn in range(ITERS):
        sum_finish(turn)
    cam_step_ref[...] = cam_step
    for j, row in enumerate(apply_three(inverse, rows_of(point_total, 3))):
        point_step_ref[j : j + 1, :] = -row


def local(groups, regions, cam_jacobian, point_jacobian, residuals, obs_camera, obs_point):
    count = obs_camera.shape[0]
    tiles = count // LANES
    blocks = 3 * groups
    inner = inner_regions(regions)
    phases = 2 * ITERS + 1
    groups_wide = groups * C_DEV
    f32, bf16 = jnp.float32, jnp.bfloat16
    near = blocks - 1
    return pl.pallas_call(
        functools.partial(kernel, groups, regions),
        out_shape=(
            jax.ShapeDtypeStruct((9, C_DEV), f32),
            jax.ShapeDtypeStruct((3, P_DEV), f32),
        ),
        in_specs=[pl.BlockSpec(memory_space=pltpu.HBM)] * 5,
        out_specs=[pl.BlockSpec(memory_space=pltpu.VMEM)] * 2,
        scratch_shapes=[
            pltpu.VMEM(cam_jacobian.shape, bf16),
            pltpu.VMEM(point_jacobian.shape, bf16),
            pltpu.VMEM(residuals.shape, f32),
            pltpu.VMEM((tiles, LANES), jnp.int32),
            pltpu.VMEM((tiles, LANES), jnp.int32),
            pltpu.VMEM((18 * tiles, LANES), f32),
            pltpu.VMEM((6 * tiles, LANES), f32),
            pltpu.VMEM((2 * tiles, LANES), f32),
            pltpu.VMEM((count, groups_wide), bf16),
            pltpu.VMEM((count, P_DEV), bf16),
            pltpu.VMEM((tiles * ROWS, LANES), f32),
            pltpu.VMEM((3, ROWS, count), bf16),
            pltpu.VMEM((tiles * NORMAL_ROWS, LANES), f32),
            pltpu.VMEM((9, 9, C_DEV), f32),
            pltpu.VMEM((blocks, NORMAL_ROWS, C_DEV), f32),
            pltpu.VMEM((blocks, NORMAL_ROWS, C_DEV), f32),
            pltpu.VMEM((ITERS, blocks, ROWS, C_DEV), f32),
            pltpu.VMEM((ITERS, blocks, 9, C_DEV), f32),
            pltpu.VMEM((ITERS, blocks, 9, C_DEV), f32),
            pltpu.VMEM((ITERS, groups * inner, 1, LANES), f32),
            pltpu.VMEM((ITERS, regions // inner, 1, LANES), f32),
            pltpu.SemaphoreType.DMA((phases, near)),
            pltpu.SemaphoreType.DMA((phases, near)),
            pltpu.SemaphoreType.DMA((2, ITERS)),
            pltpu.SemaphoreType.DMA((2, ITERS)),
            pltpu.SemaphoreType.DMA((5,)),
        ],
        compiler_params=pltpu.CompilerParams(
            collective_id=0, has_side_effects=True, vmem_limit_bytes=56 * 1024 * 1024
        ),
    )(
        cam_jacobian,
        point_jacobian,
        residuals,
        obs_camera.reshape(tiles, LANES),
        obs_point.reshape(tiles, LANES),
    )


def solution(mesh):
    placed = (
        P(None, ("grp", "reg")),
        P(None, ("grp", "reg")),
        P(None, ("grp", "reg")),
        P(("grp", "reg")),
        P(("grp", "reg")),
    )
    return jax.shard_map(
        functools.partial(local, mesh.shape["grp"], mesh.shape["reg"]),
        mesh=mesh,
        in_specs=placed,
        out_specs=(P(None, ("grp", "reg")), P(None, ("grp", "reg"))),
        check_vma=False,
    )
```

```python
import functools

import jax
import jax.numpy as jnp
from jax import lax
from jax.experimental import pallas as pl
from jax.experimental.pallas import tpu as pltpu
from jax.sharding import PartitionSpec as P

C_DEV = 128
P_DEV = 256
ITERS = 3
DAMPING = 4.0

LANES = 128
ROWS = 16
PAIRS = [(i, j) for i in range(9) for j in range(i + 1)]
NORMAL_ROWS = 48
PARTS = 3
CAMERA_PARTS = 2
POINT_PARTS = 2
HALVES = 2
MESH = pl.DeviceIdType.MESH


def split(x, count):
    parts = []
    for _ in range(count - 1):
        part = x.astype(jnp.bfloat16).astype(jnp.float32)
        parts.append(part)
        x = x - part
    parts.append(x)
    return jnp.concatenate(parts, 0).astype(jnp.bfloat16)


def product(left, onehot):
    run = onehot.shape[0] // HALVES
    total = None
    for n in range(HALVES):
        at = slice(n * run, (n + 1) * run)
        part = jnp.dot(left[:, at], onehot[at], preferred_element_type=jnp.float32)
        total = part if total is None else total + part
    return total


def sum_parts(summed, count):
    rows = summed.shape[0] // count
    total = summed[(count - 1) * rows :]
    for part in range(count - 2, -1, -1):
        total = total + summed[part * rows : (part + 1) * rows]
    return total


def sum_into(terms, onehot, count=PARTS):
    return sum_parts(product(split(terms, count), onehot), count)


def sum_near(terms, masks, onehot, count=CAMERA_PARTS):
    parts = split(terms, count)
    masked = []
    for mask in masks:
        masked.append(parts * jnp.concatenate([mask] * (parts.shape[0] // mask.shape[0]), 0))
    summed = product(jnp.concatenate(masked, 0), onehot)
    rows = parts.shape[0]
    return [sum_parts(summed[n * rows : (n + 1) * rows], count) for n in range(len(masks))]


def inverse_three(a, b, c, e, f, i):
    adjoint = [e * i - f * f, c * f - b * i, b * f - c * e, a * i - c * c, b * c - a * f, a * e - b * b]
    determinant = a * adjoint[0] + b * adjoint[1] + c * adjoint[2]
    return [entry / determinant for entry in adjoint]


def apply_three(inverse, vector):
    a, b, c, e, f, i = inverse
    x, y, z = vector
    return [a * x + b * y + c * z, b * x + e * y + f * z, c * x + f * y + i * z]


def block_inverse(entry):
    work = {(i, j): entry(i, j) for i, j in PAIRS}
    for p in range(9):
        scale = 1.0 / work[p, p]
        column = [work[max(i, p), min(i, p)] for i in range(9)]
        scaled = [value * scale for value in column]
        for i, j in PAIRS:
            if i == p and j == p:
                work[i, j] = -scale
            elif i == p:
                work[i, j] = scaled[j]
            elif j == p:
                work[i, j] = scaled[i]
            else:
                work[i, j] = work[i, j] - column[i] * scaled[j]
    return work


def inner_regions(regions):
    return max(n for n in range(1, regions + 1) if regions % n == 0 and n * n <= regions)


def kernel(
    groups,
    regions,
    cam_in,
    point_in,
    res_in,
    camera_in,
    slot_in,
    cam_step_ref,
    point_step_ref,
    cam_ref,
    point_ref,
    res_ref,
    camera_ref,
    slot_ref,
    cam_store,
    point_store,
    res_store,
    cam_hot,
    point_hot,
    stage,
    point_stage,
    near_mask,
    normal_stage,
    solve,
    normal_part,
    normal_recv,
    part,
    recv,
    table,
    first_sums,
    second_sums,
    last_sums,
    near_send,
    near_recv,
    sum_send,
    sum_recv,
    load,
):
    group = lax.axis_index("grp")
    region = lax.axis_index("reg")
    blocks = 3 * groups
    tiles = camera_ref.shape[0]

    loads = [
        pltpu.make_async_copy(source, target, load.at[n])
        for n, (source, target) in enumerate(
            [
                (camera_in, camera_ref),
                (slot_in, slot_ref),
                (cam_in, cam_ref),
                (point_in, point_ref),
                (res_in, res_ref),
            ]
        )
    ]
    for copy in loads:
        copy.start()

    def turned(position, step, size):
        return lax.select(position + step >= size, position + step - size, position + step)

    inner = inner_regions(regions)
    outer = regions // inner
    within = lax.rem(region, inner)
    plane = region // inner
    others_group = [turned(group, j, groups) for j in range(groups)]
    others_within = [turned(within, j, inner) for j in range(inner)]
    others_plane = [turned(plane, j, outer) for j in range(outer)]
    first_level = [(g, plane * inner + r) for r in others_within for g in others_group][1:]
    second_level = [(group, p * inner + within) for p in others_plane][1:]
    first_me = group * inner + within
    everyone = [(g, r) for r in [turned(region, j, regions) for j in range(regions)] for g in others_group][1:]
    me = group * regions + region

    barrier = pltpu.get_barrier_semaphore()
    for other in everyone:
        pl.semaphore_signal(barrier, inc=1, device_id=other, device_id_type=MESH)
    greeted = len(everyone)

    mine = groups + group
    has_below, has_above = region > 0, region < regions - 1

    class Near:
        def __init__(self, phase, source, target):
            self.copies = [[], [], []]
            n = 0
            for offset in range(3):
                for j in range(1 if offset == 1 else 0, groups):
                    other = others_group[j]
                    self.copies[offset].append(
                        pltpu.make_async_remote_copy(
                            src_ref=source(offset * groups + other),
                            dst_ref=target((2 - offset) * groups + group),
                            send_sem=near_send.at[phase, n],
                            recv_sem=near_recv.at[phase, n],
                            device_id=(other, turned(region, (offset - 1) % regions, regions)),
                            device_id_type=MESH,
                        )
                    )
                    n += 1

        def each(self, below, above, act):
            @pl.when(has_below)
            def _():
                for copy in self.copies[below]:
                    act(copy)

            @pl.when(has_above)
            def _():
                for copy in self.copies[above]:
                    act(copy)

            for copy in self.copies[1]:
                act(copy)

        def start(self):
            self.each(0, 2, lambda copy: copy.start())
            return self

        def wait(self):
            self.each(2, 0, lambda copy: copy.wait_recv())

        def wait_from(self, offset):
            if offset == 1:
                for copy in self.copies[1]:
                    copy.wait_recv()
                return

            @pl.when(has_below if offset == 0 else has_above)
            def _():
                for copy in self.copies[2 - offset]:
                    copy.wait_recv()

        def finish(self):
            self.each(0, 2, lambda copy: copy.wait_send())

    def clear_ends(ref):
        @pl.when(region == 0)
        def _():
            for j in range(groups):
                ref[j] = jnp.zeros(ref.shape[1:], jnp.float32)

        @pl.when(region == regions - 1)
        def _():
            for j in range(groups):
                ref[2 * groups + j] = jnp.zeros(ref.shape[1:], jnp.float32)

    def push(ref, at, others, level, phase):
        for other in others:
            pltpu.make_async_remote_copy(
                src_ref=ref.at[phase, at],
                dst_ref=ref.at[phase, at],
                send_sem=sum_send.at[level, phase],
                recv_sem=sum_recv.at[level, phase],
                device_id=other,
                device_id_type=MESH,
            ).start()

    def pulled(ref, count, level, phase):
        bytes_of = ref.at[phase, pl.ds(0, count)]
        pltpu.make_async_copy(bytes_of, bytes_of, sum_recv.at[level, phase]).wait()
        return jnp.sum(ref[phase], axis=0)

    def sum_start(phase, row):
        if phase == ITERS - 1:
            last_sums[0, me] = row
            push(last_sums, me, everyone, 2, 0)
            return
        first_sums[phase, first_me] = row
        push(first_sums, first_me, first_level, 0, phase)

    def sum_middle(phase):
        second_sums[phase, plane] = pulled(first_sums, len(first_level), 0, phase)
        push(second_sums, plane, second_level, 1, phase)

    def sum_wait(phase):
        if phase == ITERS - 1:
            sums = pulled(last_sums, len(everyone), 2, 0)
        else:
            sums = pulled(second_sums, len(second_level), 1, phase)
        return [sums[:, n : n + 1] for n in range(3)]

    def sum_finish(phase):
        levels = [(0, first_sums, first_level), (1, second_sums, second_level)]
        if phase == ITERS - 1:
            phase, levels = 0, [(2, last_sums, everyone)]
        for level, ref, others in levels:
            bytes_of = ref.at[phase, pl.ds(0, len(others))]
            pltpu.make_async_copy(bytes_of, bytes_of, sum_send.at[level, phase]).wait()

    clear_ends(normal_recv)
    for turn in range(ITERS):
        clear_ends(table.at[turn])
        clear_ends(recv.at[turn])
    stage[...] = jnp.zeros_like(stage)
    point_stage[...] = jnp.zeros_like(point_stage)
    normal_stage[...] = jnp.zeros_like(normal_stage)

    for copy in loads[:2]:
        copy.wait()
    camera = camera_ref[...]
    owner = jnp.right_shift(camera, C_DEV.bit_length() - 1)
    lane = jnp.bitwise_and(camera, C_DEV - 1)
    owner_group = jnp.zeros_like(owner)
    for j in range(1, groups):
        owner_group = owner_group + jnp.where(owner >= j * regions, 1, 0)
    offset_of = owner - owner_group * regions - region + 1
    block_of = offset_of * groups + owner_group
    for n in range(3):
        here = jnp.where(offset_of == n, 1.0, 0.0)
        for s in range(tiles):
            row = jnp.broadcast_to(here[s : s + 1], (ROWS, LANES))
            near_mask[n, :, s * LANES : (s + 1) * LANES] = row.astype(jnp.bfloat16)
    slot = slot_ref[...]
    point_lane = jnp.bitwise_and(slot, LANES - 1)
    point_tile = jnp.right_shift(slot, LANES.bit_length() - 1)

    column_t = jnp.transpose((owner_group * C_DEV + lane).astype(jnp.float32))
    cam_iota = lax.broadcasted_iota(jnp.int32, (LANES, groups * C_DEV), 1).astype(jnp.float32)
    for s in range(tiles):
        at = slice(s * LANES, (s + 1) * LANES)
        cam_hot[at, :] = jnp.where(column_t[:, s : s + 1] == cam_iota, 1.0, 0.0).astype(jnp.bfloat16)

    for copy in loads[2:]:
        copy.wait()
    for s in range(tiles):
        lanes = slice(s * LANES, (s + 1) * LANES)
        cam_store[pl.ds(s, 18, stride=tiles), :] = cam_ref[:, lanes].astype(jnp.float32)
        point_store[pl.ds(s, 6, stride=tiles), :] = point_ref[:, lanes].astype(jnp.float32)
        res_store[pl.ds(s, 2, stride=tiles), :] = res_ref[:, lanes]
    cam_rows = [cam_store[n * tiles : (n + 1) * tiles] for n in range(18)]
    point_rows = [point_store[n * tiles : (n + 1) * tiles] for n in range(6)]
    residuals = [res_store[n * tiles : (n + 1) * tiles] for n in range(2)]

    def put(ref, row, term):
        ref[pl.ds(row, tiles, stride=ref.shape[0] // tiles), :] = term

    def staged(ref):
        rows = ref.shape[0] // tiles
        return jnp.concatenate([ref[s * rows : (s + 1) * rows] for s in range(tiles)], 1)

    def pick(rows, tile, at):
        total = None
        for n, row in enumerate(rows):
            wide = jnp.broadcast_to(row, (tiles, LANES))
            got = jnp.take_along_axis(wide, at, axis=1, mode="promise_in_bounds")
            total = got if total is None else jnp.where(tile == n, got, total)
        return total

    def point_terms(values, stage):
        for j in range(3):
            put(stage, j, point_rows[j] * values[0] + point_rows[3 + j] * values[1])

    masks = [near_mask.at[n] for n in range(3)]

    def by_block(ref, summed):
        for n in range(3):
            for j in range(groups):
                ref[n * groups + j] = summed[n][:, j * C_DEV : (j + 1) * C_DEV]

    def rows_of(block, count):
        return [block[j : j + 1] for j in range(count)]

    def remains(values, gathered):
        solved = apply_three(inverse, rows_of(gathered, 3))
        picked = [
            pick([row[:, n * LANES : (n + 1) * LANES] for n in range(P_DEV // LANES)], point_tile, point_lane)
            for row in solved
        ]
        return [
            values[i]
            - (
                point_rows[3 * i] * picked[0]
                + point_rows[3 * i + 1] * picked[1]
                + point_rows[3 * i + 2] * picked[2]
            )
            for i in range(2)
        ]

    for n, (i, j) in enumerate(PAIRS):
        put(normal_stage, n, cam_rows[i] * cam_rows[j] + cam_rows[9 + i] * cam_rows[9 + j])
    by_block(
        normal_part,
        sum_near(staged(normal_stage), [mask[...] for mask in masks], cam_hot[...]),
    )
    pl.semaphore_wait(barrier, greeted)
    normal = Near(0, lambda block: normal_part.at[block], lambda at: normal_recv.at[at]).start()
    normal_recv[mine] = normal_part[mine]

    slot_t = jnp.transpose(slot.astype(jnp.float32))
    point_iota = lax.broadcasted_iota(jnp.int32, (LANES, P_DEV), 1).astype(jnp.float32)
    for s in range(tiles):
        at = slice(s * LANES, (s + 1) * LANES)
        point_hot[at, :] = jnp.where(slot_t[:, s : s + 1] == point_iota, 1.0, 0.0).astype(jnp.bfloat16)
    first = [residuals[0], residuals[1]]
    point_terms(first, stage)
    for n, (i, j) in enumerate([(0, 0), (0, 1), (0, 2), (1, 1), (1, 2), (2, 2)]):
        put(stage, 3 + n, point_rows[i] * point_rows[j] + point_rows[3 + i] * point_rows[3 + j])
    sums = sum_into(staged(stage), point_hot[...])
    entries = rows_of(sums[3:9], 6)
    for n in (0, 3, 5):
        entries[n] = entries[n] + DAMPING
    inverse = inverse_three(*entries)
    point_total = sums[:8]

    def send_back(phase, at, remain):
        for k in range(9):
            put(stage, k, cam_rows[k] * remain[0] + cam_rows[9 + k] * remain[1])
        by_block(part.at[at], sum_near(staged(stage), [mask[...] for mask in masks], cam_hot[...]))
        back = Near(
            phase, lambda block: part.at[at, block, pl.ds(0, 9)], lambda block: recv.at[at, block]
        ).start()
        recv[at, mine] = part[at, mine, :9]
        return back

    def taken_back(at):
        out = recv[at, 0]
        for n in range(1, blocks):
            out = out + recv[at, n]
        return out

    gradient = send_back(1, ITERS - 1, remains(first, sums))
    normal.wait()
    total = normal_recv[0]
    for n in range(1, blocks):
        total = total + normal_recv[n]

    def entry(i, j):
        n = PAIRS.index((i, j))
        row = total[n : n + 1]
        return row + DAMPING if i == j else row

    minus_inverse = block_inverse(entry)
    for i, j in PAIRS:
        solve[i, j : j + 1, :] = -minus_inverse[i, j]
        if i != j:
            solve[j, i : i + 1, :] = -minus_inverse[i, j]

    def precondition(field):
        out = solve[0] * field[0:1]
        for k in range(1, 9):
            out = out + solve[k] * field[k : k + 1]
        return out

    def dot(x, y):
        return jnp.sum(x * y, axis=0, keepdims=True)

    def moved(x, scale, y):
        return [a + scale * b for a, b in zip(x, y)]

    gradient.wait()
    exchanges = [normal, gradient]
    lanes_of = lax.broadcasted_iota(jnp.int32, (1, LANES), 1)
    residual = -taken_back(ITERS - 1)
    field = precondition(residual)
    cam_step = jnp.zeros((9, C_DEV), jnp.float32)
    z = direction = slope = image = product = current = curvature = None
    for turn in range(ITERS):
        table[turn, mine] = field
        spread = Near(
            2 + 2 * turn, lambda block: table.at[turn, mine], lambda at: table.at[turn, at]
        ).start()
        exchanges.append(spread)
        picked = [None] * 9
        for offset in (1, 0, 2):
            spread.wait_from(offset)
            for n in range(offset * groups, (offset + 1) * groups):
                for k in range(9):
                    row = jnp.broadcast_to(table[turn, n, k : k + 1], (tiles, LANES))
                    got = jnp.take_along_axis(row, lane, axis=1, mode="promise_in_bounds")
                    picked[k] = got if picked[k] is None else jnp.where(block_of == n, got, picked[k])
        if turn > 0:
            following, energy, cross = sum_wait(turn - 1)
        values = [None, None]
        for k in range(9):
            for i in range(2):
                term = cam_rows[9 * i + k] * picked[k]
                values[i] = term if k == 0 else values[i] + term
        point_terms(values, point_stage)
        fresh = [field] + values + [sum_into(staged(point_stage), point_hot[...], POINT_PARTS)]
        if turn == 0:
            z = fresh
        else:
            if turn == 1:
                curvature, direction, slope, image = energy, [z[0], z[3]], fresh, product
            else:
                ratio = following / current
                curvature = energy + ratio * (2.0 * cross + ratio * curvature)
                direction = moved([z[0], z[3]], ratio, direction)
                slope = moved(fresh, ratio, slope)
                image = product + ratio * image
            current = following
            step_size = current / curvature
            cam_step = cam_step + step_size * direction[0]
            point_total = point_total + step_size * direction[1]
            residual = residual - step_size * image
            z = moved(z, -step_size, slope)
        remain = remains(z[1:3], z[3])
        sums_of = [
            dot(residual, z[0]),
            DAMPING * dot(z[0], z[0]) + dot(z[1], remain[0]) + dot(z[2], remain[1]),
            jnp.zeros((1, LANES), jnp.float32) if turn == 0 else dot(z[0], image),
        ]
        sums_of = [jnp.sum(x, axis=1, keepdims=True) for x in sums_of]
        sum_start(turn, jnp.where(lanes_of == 0, sums_of[0], jnp.where(lanes_of == 1, sums_of[1], sums_of[2])))
        if turn + 1 < ITERS:
            back = send_back(3 + 2 * turn, turn, remain)
            exchanges.append(back)
            back.wait()
            sum_middle(turn)
            product = DAMPING * z[0] + taken_back(turn)
            field = precondition(product)

    following, energy, cross = sum_wait(ITERS - 1)
    ratio = following / current
    curvature = energy + ratio * (2.0 * cross + ratio * curvature)
    direction = moved([z[0], z[3]], ratio, direction)
    step_size = following / curvature
    cam_step = cam_step + step_size * direction[0]
    point_total = point_total + step_size * direction[1]
    for exchange in exchanges:
        exchange.finish()
    for turn in range(ITERS):
        sum_finish(turn)
    cam_step_ref[...] = cam_step
    for j, row in enumerate(apply_three(inverse, rows_of(point_total, 3))):
        point_step_ref[j : j + 1, :] = -row


def local(groups, regions, cam_jacobian, point_jacobian, residuals, obs_camera, obs_point):
    count = obs_camera.shape[0]
    tiles = count // LANES
    blocks = 3 * groups
    inner = inner_regions(regions)
    phases = 2 * ITERS + 1
    groups_wide = groups * C_DEV
    f32, bf16 = jnp.float32, jnp.bfloat16
    near = blocks - 1
    return pl.pallas_call(
        functools.partial(kernel, groups, regions),
        out_shape=(
            jax.ShapeDtypeStruct((9, C_DEV), f32),
            jax.ShapeDtypeStruct((3, P_DEV), f32),
        ),
        in_specs=[pl.BlockSpec(memory_space=pltpu.HBM)] * 5,
        out_specs=[pl.BlockSpec(memory_space=pltpu.VMEM)] * 2,
        scratch_shapes=[
            pltpu.VMEM(cam_jacobian.shape, bf16),
            pltpu.VMEM(point_jacobian.shape, bf16),
            pltpu.VMEM(residuals.shape, f32),
            pltpu.VMEM((tiles, LANES), jnp.int32),
            pltpu.VMEM((tiles, LANES), jnp.int32),
            pltpu.VMEM((18 * tiles, LANES), f32),
            pltpu.VMEM((6 * tiles, LANES), f32),
            pltpu.VMEM((2 * tiles, LANES), f32),
            pltpu.VMEM((count, groups_wide), bf16),
            pltpu.VMEM((count, P_DEV), bf16),
            pltpu.VMEM((tiles * ROWS, LANES), f32),
            pltpu.VMEM((tiles * 8, LANES), f32),
            pltpu.VMEM((3, ROWS, count), bf16),
            pltpu.VMEM((tiles * NORMAL_ROWS, LANES), f32),
            pltpu.VMEM((9, 9, C_DEV), f32),
            pltpu.VMEM((blocks, NORMAL_ROWS, C_DEV), f32),
            pltpu.VMEM((blocks, NORMAL_ROWS, C_DEV), f32),
            pltpu.VMEM((ITERS, blocks, ROWS, C_DEV), f32),
            pltpu.VMEM((ITERS, blocks, 9, C_DEV), f32),
            pltpu.VMEM((ITERS, blocks, 9, C_DEV), f32),
            pltpu.VMEM((ITERS - 1, groups * inner, 1, LANES), f32),
            pltpu.VMEM((ITERS - 1, regions // inner, 1, LANES), f32),
            pltpu.VMEM((1, groups * regions, 1, LANES), f32),
            pltpu.SemaphoreType.DMA((phases, near)),
            pltpu.SemaphoreType.DMA((phases, near)),
            pltpu.SemaphoreType.DMA((3, ITERS)),
            pltpu.SemaphoreType.DMA((3, ITERS)),
            pltpu.SemaphoreType.DMA((5,)),
        ],
        compiler_params=pltpu.CompilerParams(
            collective_id=0, has_side_effects=True, vmem_limit_bytes=56 * 1024 * 1024
        ),
    )(
        cam_jacobian,
        point_jacobian,
        residuals,
        obs_camera.reshape(tiles, LANES),
        obs_point.reshape(tiles, LANES),
    )


def solution(mesh):
    placed = (
        P(None, ("grp", "reg")),
        P(None, ("grp", "reg")),
        P(None, ("grp", "reg")),
        P(("grp", "reg")),
        P(("grp", "reg")),
    )
    return jax.shard_map(
        functools.partial(local, mesh.shape["grp"], mesh.shape["reg"]),
        mesh=mesh,
        in_specs=placed,
        out_specs=(P(None, ("grp", "reg")), P(None, ("grp", "reg"))),
        check_vma=False,
    )
```

```python
import functools

import jax
import jax.numpy as jnp
from jax import lax
from jax.experimental import pallas as pl
from jax.experimental.pallas import tpu as pltpu
from jax.sharding import PartitionSpec as P

C_DEV = 128
P_DEV = 256
ITERS = 3
DAMPING = 4.0

LANES = 128
ROWS = 16
PAIRS = [(i, j) for i in range(9) for j in range(i + 1)]
NORMAL_ROWS = 48
PARTS = 3
CAMERA_PARTS = 2
POINT_PARTS = 2
HALVES = 2
MESH = pl.DeviceIdType.MESH


def split(x, count):
    parts = []
    for _ in range(count - 1):
        part = x.astype(jnp.bfloat16).astype(jnp.float32)
        parts.append(part)
        x = x - part
    parts.append(x)
    return jnp.concatenate(parts, 0).astype(jnp.bfloat16)


def product(left, onehot):
    run = onehot.shape[0] // HALVES
    total = None
    for n in range(HALVES):
        at = slice(n * run, (n + 1) * run)
        part = jnp.dot(left[:, at], onehot[at], preferred_element_type=jnp.float32)
        total = part if total is None else total + part
    return total


def sum_parts(summed, count):
    rows = summed.shape[0] // count
    total = summed[(count - 1) * rows :]
    for part in range(count - 2, -1, -1):
        total = total + summed[part * rows : (part + 1) * rows]
    return total


def sum_into(terms, onehot, count=PARTS):
    return sum_parts(product(split(terms, count), onehot), count)


def sum_near(terms, masks, onehot, count=CAMERA_PARTS):
    parts = split(terms, count)
    masked = []
    for mask in masks:
        masked.append(parts * jnp.concatenate([mask] * (parts.shape[0] // mask.shape[0]), 0))
    summed = product(jnp.concatenate(masked, 0), onehot)
    rows = parts.shape[0]
    return [sum_parts(summed[n * rows : (n + 1) * rows], count) for n in range(len(masks))]


def inverse_three(a, b, c, e, f, i):
    adjoint = [e * i - f * f, c * f - b * i, b * f - c * e, a * i - c * c, b * c - a * f, a * e - b * b]
    determinant = a * adjoint[0] + b * adjoint[1] + c * adjoint[2]
    return [entry / determinant for entry in adjoint]


def apply_three(inverse, vector):
    a, b, c, e, f, i = inverse
    x, y, z = vector
    return [a * x + b * y + c * z, b * x + e * y + f * z, c * x + f * y + i * z]


def block_inverse(entry):
    work = {(i, j): entry(i, j) for i, j in PAIRS}
    for p in range(9):
        scale = 1.0 / work[p, p]
        column = [work[max(i, p), min(i, p)] for i in range(9)]
        scaled = [value * scale for value in column]
        for i, j in PAIRS:
            if i == p and j == p:
                work[i, j] = -scale
            elif i == p:
                work[i, j] = scaled[j]
            elif j == p:
                work[i, j] = scaled[i]
            else:
                work[i, j] = work[i, j] - column[i] * scaled[j]
    return work


def inner_regions(regions):
    return max(n for n in range(1, regions + 1) if regions % n == 0 and n * n <= regions)


def kernel(
    groups,
    regions,
    cam_in,
    point_in,
    res_in,
    camera_in,
    slot_in,
    cam_step_ref,
    point_step_ref,
    cam_ref,
    point_ref,
    res_ref,
    camera_ref,
    slot_ref,
    cam_store,
    point_store,
    res_store,
    cam_hot,
    point_hot,
    stage,
    point_stage,
    near_mask,
    normal_stage,
    solve,
    normal_part,
    normal_recv,
    part,
    recv,
    table,
    first_sums,
    second_sums,
    last_sums,
    near_send,
    near_recv,
    sum_send,
    sum_recv,
    load,
):
    group = lax.axis_index("grp")
    region = lax.axis_index("reg")
    blocks = 3 * groups
    tiles = camera_ref.shape[0]

    loads = [
        pltpu.make_async_copy(source, target, load.at[n])
        for n, (source, target) in enumerate(
            [
                (camera_in, camera_ref),
                (slot_in, slot_ref),
                (cam_in, cam_ref),
                (point_in, point_ref),
                (res_in, res_ref),
            ]
        )
    ]
    for copy in loads:
        copy.start()

    def turned(position, step, size):
        return lax.select(position + step >= size, position + step - size, position + step)

    inner = inner_regions(regions)
    outer = regions // inner
    within = lax.rem(region, inner)
    plane = region // inner
    others_group = [turned(group, j, groups) for j in range(groups)]
    others_within = [turned(within, j, inner) for j in range(inner)]
    others_plane = [turned(plane, j, outer) for j in range(outer)]
    first_level = [(g, plane * inner + r) for r in others_within for g in others_group][1:]
    second_level = [(group, p * inner + within) for p in others_plane][1:]
    first_me = group * inner + within
    everyone = [(g, r) for r in [turned(region, j, regions) for j in range(regions)] for g in others_group][1:]
    me = group * regions + region

    barrier = pltpu.get_barrier_semaphore()
    for other in everyone:
        pl.semaphore_signal(barrier, inc=1, device_id=other, device_id_type=MESH)
    greeted = len(everyone)

    mine = groups + group
    has_below, has_above = region > 0, region < regions - 1

    class Near:
        def __init__(self, phase, source, target):
            self.copies = [[], [], []]
            n = 0
            for offset in range(3):
                for j in range(1 if offset == 1 else 0, groups):
                    other = others_group[j]
                    self.copies[offset].append(
                        pltpu.make_async_remote_copy(
                            src_ref=source(offset * groups + other),
                            dst_ref=target((2 - offset) * groups + group),
                            send_sem=near_send.at[phase, n],
                            recv_sem=near_recv.at[phase, n],
                            device_id=(other, turned(region, (offset - 1) % regions, regions)),
                            device_id_type=MESH,
                        )
                    )
                    n += 1

        def each(self, below, above, act):
            @pl.when(has_below)
            def _():
                for copy in self.copies[below]:
                    act(copy)

            @pl.when(has_above)
            def _():
                for copy in self.copies[above]:
                    act(copy)

            for copy in self.copies[1]:
                act(copy)

        def start(self):
            self.each(0, 2, lambda copy: copy.start())
            return self

        def wait(self):
            self.each(2, 0, lambda copy: copy.wait_recv())

        def wait_from(self, offset):
            if offset == 1:
                for copy in self.copies[1]:
                    copy.wait_recv()
                return

            @pl.when(has_below if offset == 0 else has_above)
            def _():
                for copy in self.copies[2 - offset]:
                    copy.wait_recv()

        def finish(self):
            self.each(0, 2, lambda copy: copy.wait_send())

    def clear_ends(ref):
        @pl.when(region == 0)
        def _():
            for j in range(groups):
                ref[j] = jnp.zeros(ref.shape[1:], jnp.float32)

        @pl.when(region == regions - 1)
        def _():
            for j in range(groups):
                ref[2 * groups + j] = jnp.zeros(ref.shape[1:], jnp.float32)

    def push(ref, at, others, level, phase):
        for other in others:
            pltpu.make_async_remote_copy(
                src_ref=ref.at[phase, at],
                dst_ref=ref.at[phase, at],
                send_sem=sum_send.at[level, phase],
                recv_sem=sum_recv.at[level, phase],
                device_id=other,
                device_id_type=MESH,
            ).start()

    def pulled(ref, count, level, phase):
        bytes_of = ref.at[phase, pl.ds(0, count)]
        pltpu.make_async_copy(bytes_of, bytes_of, sum_recv.at[level, phase]).wait()
        return jnp.sum(ref[phase], axis=0)

    def sum_start(phase, row):
        if phase == ITERS - 1:
            last_sums[0, me] = row
            push(last_sums, me, everyone, 2, 0)
            return
        first_sums[phase, first_me] = row
        push(first_sums, first_me, first_level, 0, phase)

    def sum_middle(phase):
        second_sums[phase, plane] = pulled(first_sums, len(first_level), 0, phase)
        push(second_sums, plane, second_level, 1, phase)

    def sum_wait(phase):
        if phase == ITERS - 1:
            sums = pulled(last_sums, len(everyone), 2, 0)
        else:
            sums = pulled(second_sums, len(second_level), 1, phase)
        return [sums[:, n : n + 1] for n in range(3)]

    def sum_finish(phase):
        levels = [(0, first_sums, first_level), (1, second_sums, second_level)]
        if phase == ITERS - 1:
            phase, levels = 0, [(2, last_sums, everyone)]
        for level, ref, others in levels:
            bytes_of = ref.at[phase, pl.ds(0, len(others))]
            pltpu.make_async_copy(bytes_of, bytes_of, sum_send.at[level, phase]).wait()

    clear_ends(normal_recv)
    for turn in range(ITERS):
        clear_ends(table.at[turn])
        clear_ends(recv.at[turn])
    stage[...] = jnp.zeros_like(stage)
    point_stage[...] = jnp.zeros_like(point_stage)
    normal_stage[...] = jnp.zeros_like(normal_stage)

    for copy in loads[:2]:
        copy.wait()
    camera = camera_ref[...]
    owner = jnp.right_shift(camera, C_DEV.bit_length() - 1)
    lane = jnp.bitwise_and(camera, C_DEV - 1)
    owner_group = jnp.zeros_like(owner)
    for j in range(1, groups):
        owner_group = owner_group + jnp.where(owner >= j * regions, 1, 0)
    offset_of = owner - owner_group * regions - region + 1
    block_of = offset_of * groups + owner_group
    for n in range(3):
        here = jnp.where(offset_of == n, 1.0, 0.0)
        for s in range(tiles):
            row = jnp.broadcast_to(here[s : s + 1], (ROWS, LANES))
            near_mask[n, :, s * LANES : (s + 1) * LANES] = row.astype(jnp.bfloat16)
    slot = slot_ref[...]
    point_lane = jnp.bitwise_and(slot, LANES - 1)
    point_tile = jnp.right_shift(slot, LANES.bit_length() - 1)

    column_t = jnp.transpose((owner_group * C_DEV + lane).astype(jnp.float32))
    cam_iota = lax.broadcasted_iota(jnp.int32, (LANES, groups * C_DEV), 1).astype(jnp.float32)
    for s in range(tiles):
        at = slice(s * LANES, (s + 1) * LANES)
        cam_hot[at, :] = jnp.where(column_t[:, s : s + 1] == cam_iota, 1.0, 0.0).astype(jnp.bfloat16)

    for copy in loads[2:]:
        copy.wait()
    for s in range(tiles):
        lanes = slice(s * LANES, (s + 1) * LANES)
        cam_store[pl.ds(s, 18, stride=tiles), :] = cam_ref[:, lanes].astype(jnp.float32)
        point_store[pl.ds(s, 6, stride=tiles), :] = point_ref[:, lanes].astype(jnp.float32)
        res_store[pl.ds(s, 2, stride=tiles), :] = res_ref[:, lanes]
    cam_rows = [cam_store[n * tiles : (n + 1) * tiles] for n in range(18)]
    point_rows = [point_store[n * tiles : (n + 1) * tiles] for n in range(6)]
    residuals = [res_store[n * tiles : (n + 1) * tiles] for n in range(2)]

    def put(ref, row, term):
        ref[pl.ds(row, tiles, stride=ref.shape[0] // tiles), :] = term

    def staged(ref):
        rows = ref.shape[0] // tiles
        return jnp.concatenate([ref[s * rows : (s + 1) * rows] for s in range(tiles)], 1)

    def pick(rows, tile, at):
        total = None
        for n, row in enumerate(rows):
            wide = jnp.broadcast_to(row, (tiles, LANES))
            got = jnp.take_along_axis(wide, at, axis=1, mode="promise_in_bounds")
            total = got if total is None else jnp.where(tile == n, got, total)
        return total

    def point_terms(values, stage):
        for j in range(3):
            put(stage, j, point_rows[j] * values[0] + point_rows[3 + j] * values[1])

    masks = [near_mask.at[n] for n in range(3)]

    def by_block(ref, summed):
        for n in range(3):
            for j in range(groups):
                ref[n * groups + j] = summed[n][:, j * C_DEV : (j + 1) * C_DEV]

    def rows_of(block, count):
        return [block[j : j + 1] for j in range(count)]

    def remains(values, gathered):
        solved = apply_three(inverse, rows_of(gathered, 3))
        picked = [
            pick([row[:, n * LANES : (n + 1) * LANES] for n in range(P_DEV // LANES)], point_tile, point_lane)
            for row in solved
        ]
        return [
            values[i]
            - (
                point_rows[3 * i] * picked[0]
                + point_rows[3 * i + 1] * picked[1]
                + point_rows[3 * i + 2] * picked[2]
            )
            for i in range(2)
        ]

    for n, (i, j) in enumerate(PAIRS):
        put(normal_stage, n, cam_rows[i] * cam_rows[j] + cam_rows[9 + i] * cam_rows[9 + j])
    by_block(
        normal_part,
        sum_near(staged(normal_stage), [mask[...] for mask in masks], cam_hot[...]),
    )
    pl.semaphore_wait(barrier, greeted)
    normal = Near(0, lambda block: normal_part.at[block], lambda at: normal_recv.at[at]).start()
    normal_recv[mine] = normal_part[mine]

    slot_t = jnp.transpose(slot.astype(jnp.float32))
    point_iota = lax.broadcasted_iota(jnp.int32, (LANES, P_DEV), 1).astype(jnp.float32)
    for s in range(tiles):
        at = slice(s * LANES, (s + 1) * LANES)
        point_hot[at, :] = jnp.where(slot_t[:, s : s + 1] == point_iota, 1.0, 0.0).astype(jnp.bfloat16)
    first = [residuals[0], residuals[1]]
    point_terms(first, stage)
    for n, (i, j) in enumerate([(0, 0), (0, 1), (0, 2), (1, 1), (1, 2), (2, 2)]):
        put(stage, 3 + n, point_rows[i] * point_rows[j] + point_rows[3 + i] * point_rows[3 + j])
    sums = sum_into(staged(stage), point_hot[...])
    entries = rows_of(sums[3:9], 6)
    for n in (0, 3, 5):
        entries[n] = entries[n] + DAMPING
    inverse = inverse_three(*entries)
    point_total = sums[:8]

    def send_back(phase, at, remain):
        for k in range(9):
            put(stage, k, cam_rows[k] * remain[0] + cam_rows[9 + k] * remain[1])
        by_block(part.at[at], sum_near(staged(stage), [mask[...] for mask in masks], cam_hot[...]))
        back = Near(
            phase, lambda block: part.at[at, block, pl.ds(0, 9)], lambda block: recv.at[at, block]
        ).start()
        recv[at, mine] = part[at, mine, :9]
        return back

    def taken_back(at):
        out = recv[at, 0]
        for n in range(1, blocks):
            out = out + recv[at, n]
        return out

    gradient = send_back(1, ITERS - 1, remains(first, sums))
    normal.wait()
    total = normal_recv[0]
    for n in range(1, blocks):
        total = total + normal_recv[n]

    def entry(i, j):
        n = PAIRS.index((i, j))
        row = total[n : n + 1]
        return row + DAMPING if i == j else row

    minus_inverse = block_inverse(entry)
    for i, j in PAIRS:
        solve[i, j : j + 1, :] = -minus_inverse[i, j]
        if i != j:
            solve[j, i : i + 1, :] = -minus_inverse[i, j]

    def precondition(field):
        out = solve[0] * field[0:1]
        for k in range(1, 9):
            out = out + solve[k] * field[k : k + 1]
        return out

    def dot(x, y):
        return jnp.sum(x * y, axis=0, keepdims=True)

    def moved(x, scale, y):
        return [a + scale * b for a, b in zip(x, y)]

    gradient.wait()
    exchanges = [normal, gradient]
    lanes_of = lax.broadcasted_iota(jnp.int32, (1, LANES), 1)
    residual = -taken_back(ITERS - 1)
    field = precondition(residual)
    cam_step = jnp.zeros((9, C_DEV), jnp.float32)
    z = direction = slope = image = product = current = curvature = None
    for turn in range(ITERS):
        table[turn, mine] = field
        spread = Near(
            2 + 2 * turn, lambda block: table.at[turn, mine], lambda at: table.at[turn, at]
        ).start()
        exchanges.append(spread)
        if turn > 0:
            sum_middle(turn - 1)
        picked = [None] * 9
        for offset in (1, 0, 2):
            spread.wait_from(offset)
            for n in range(offset * groups, (offset + 1) * groups):
                for k in range(9):
                    row = jnp.broadcast_to(table[turn, n, k : k + 1], (tiles, LANES))
                    got = jnp.take_along_axis(row, lane, axis=1, mode="promise_in_bounds")
                    picked[k] = got if picked[k] is None else jnp.where(block_of == n, got, picked[k])
        if turn > 0:
            following, energy, cross = sum_wait(turn - 1)
        values = [None, None]
        for k in range(9):
            for i in range(2):
                term = cam_rows[9 * i + k] * picked[k]
                values[i] = term if k == 0 else values[i] + term
        point_terms(values, point_stage)
        fresh = [field] + values + [sum_into(staged(point_stage), point_hot[...], POINT_PARTS)]
        if turn == 0:
            z = fresh
        else:
            if turn == 1:
                curvature, direction, slope, image = energy, [z[0], z[3]], fresh, product
            else:
                ratio = following / current
                curvature = energy + ratio * (2.0 * cross + ratio * curvature)
                direction = moved([z[0], z[3]], ratio, direction)
                slope = moved(fresh, ratio, slope)
                image = product + ratio * image
            current = following
            step_size = current / curvature
            cam_step = cam_step + step_size * direction[0]
            point_total = point_total + step_size * direction[1]
            residual = residual - step_size * image
            z = moved(z, -step_size, slope)
        remain = remains(z[1:3], z[3])
        if turn + 1 < ITERS:
            back = send_back(3 + 2 * turn, turn, remain)
            exchanges.append(back)
        sums_of = [
            dot(residual, z[0]),
            DAMPING * dot(z[0], z[0]) + dot(z[1], remain[0]) + dot(z[2], remain[1]),
            jnp.zeros((1, LANES), jnp.float32) if turn == 0 else dot(z[0], image),
        ]
        sums_of = [jnp.sum(x, axis=1, keepdims=True) for x in sums_of]
        sum_start(turn, jnp.where(lanes_of == 0, sums_of[0], jnp.where(lanes_of == 1, sums_of[1], sums_of[2])))
        if turn + 1 < ITERS:
            back.wait()
            product = DAMPING * z[0] + taken_back(turn)
            field = precondition(product)

    for exchange in exchanges:
        exchange.finish()
    for turn in range(ITERS - 1):
        sum_finish(turn)
    following, energy, cross = sum_wait(ITERS - 1)
    ratio = following / current
    curvature = energy + ratio * (2.0 * cross + ratio * curvature)
    direction = moved([z[0], z[3]], ratio, direction)
    step_size = following / curvature
    cam_step = cam_step + step_size * direction[0]
    point_total = point_total + step_size * direction[1]
    sum_finish(ITERS - 1)
    cam_step_ref[...] = cam_step
    for j, row in enumerate(apply_three(inverse, rows_of(point_total, 3))):
        point_step_ref[j : j + 1, :] = -row


def local(groups, regions, cam_jacobian, point_jacobian, residuals, obs_camera, obs_point):
    count = obs_camera.shape[0]
    tiles = count // LANES
    blocks = 3 * groups
    inner = inner_regions(regions)
    phases = 2 * ITERS + 1
    groups_wide = groups * C_DEV
    f32, bf16 = jnp.float32, jnp.bfloat16
    near = blocks - 1
    return pl.pallas_call(
        functools.partial(kernel, groups, regions),
        out_shape=(
            jax.ShapeDtypeStruct((9, C_DEV), f32),
            jax.ShapeDtypeStruct((3, P_DEV), f32),
        ),
        in_specs=[pl.BlockSpec(memory_space=pltpu.HBM)] * 5,
        out_specs=[pl.BlockSpec(memory_space=pltpu.VMEM)] * 2,
        scratch_shapes=[
            pltpu.VMEM(cam_jacobian.shape, bf16),
            pltpu.VMEM(point_jacobian.shape, bf16),
            pltpu.VMEM(residuals.shape, f32),
            pltpu.VMEM((tiles, LANES), jnp.int32),
            pltpu.VMEM((tiles, LANES), jnp.int32),
            pltpu.VMEM((18 * tiles, LANES), f32),
            pltpu.VMEM((6 * tiles, LANES), f32),
            pltpu.VMEM((2 * tiles, LANES), f32),
            pltpu.VMEM((count, groups_wide), bf16),
            pltpu.VMEM((count, P_DEV), bf16),
            pltpu.VMEM((tiles * ROWS, LANES), f32),
            pltpu.VMEM((tiles * 8, LANES), f32),
            pltpu.VMEM((3, ROWS, count), bf16),
            pltpu.VMEM((tiles * NORMAL_ROWS, LANES), f32),
            pltpu.VMEM((9, 9, C_DEV), f32),
            pltpu.VMEM((blocks, NORMAL_ROWS, C_DEV), f32),
            pltpu.VMEM((blocks, NORMAL_ROWS, C_DEV), f32),
            pltpu.VMEM((ITERS, blocks, ROWS, C_DEV), f32),
            pltpu.VMEM((ITERS, blocks, 9, C_DEV), f32),
            pltpu.VMEM((ITERS, blocks, 9, C_DEV), f32),
            pltpu.VMEM((ITERS - 1, groups * inner, 1, LANES), f32),
            pltpu.VMEM((ITERS - 1, regions // inner, 1, LANES), f32),
            pltpu.VMEM((1, groups * regions, 1, LANES), f32),
            pltpu.SemaphoreType.DMA((phases, near)),
            pltpu.SemaphoreType.DMA((phases, near)),
            pltpu.SemaphoreType.DMA((3, ITERS)),
            pltpu.SemaphoreType.DMA((3, ITERS)),
            pltpu.SemaphoreType.DMA((5,)),
        ],
        compiler_params=pltpu.CompilerParams(
            collective_id=0, has_side_effects=True, vmem_limit_bytes=56 * 1024 * 1024
        ),
    )(
        cam_jacobian,
        point_jacobian,
        residuals,
        obs_camera.reshape(tiles, LANES),
        obs_point.reshape(tiles, LANES),
    )


def solution(mesh):
    placed = (
        P(None, ("grp", "reg")),
        P(None, ("grp", "reg")),
        P(None, ("grp", "reg")),
        P(("grp", "reg")),
        P(("grp", "reg")),
    )
    return jax.shard_map(
        functools.partial(local, mesh.shape["grp"], mesh.shape["reg"]),
        mesh=mesh,
        in_specs=placed,
        out_specs=(P(None, ("grp", "reg")), P(None, ("grp", "reg"))),
        check_vma=False,
    )
```

```python
import functools

import jax
import jax.numpy as jnp
from jax import lax
from jax.experimental import pallas as pl
from jax.experimental.pallas import tpu as pltpu
from jax.sharding import PartitionSpec as P

C_DEV = 128
P_DEV = 256
ITERS = 3
DAMPING = 4.0

LANES = 128
ROWS = 16
PAIRS = [(i, j) for i in range(9) for j in range(i + 1)]
NORMAL_ROWS = 48
PARTS = 3
CAMERA_PARTS = 2
POINT_PARTS = 2
HALVES = 4
MESH = pl.DeviceIdType.MESH


def split(x, count):
    parts = []
    for _ in range(count - 1):
        part = x.astype(jnp.bfloat16).astype(jnp.float32)
        parts.append(part)
        x = x - part
    parts.append(x)
    return jnp.concatenate(parts, 0).astype(jnp.bfloat16)


def product(left, onehot):
    run = onehot.shape[0] // HALVES
    total = None
    for n in range(HALVES):
        at = slice(n * run, (n + 1) * run)
        part = jnp.dot(left[:, at], onehot[at], preferred_element_type=jnp.float32)
        total = part if total is None else total + part
    return total


def sum_parts(summed, count):
    rows = summed.shape[0] // count
    total = summed[(count - 1) * rows :]
    for part in range(count - 2, -1, -1):
        total = total + summed[part * rows : (part + 1) * rows]
    return total


def sum_into(terms, onehot, count=PARTS):
    return sum_parts(product(split(terms, count), onehot), count)


def sum_near(terms, masks, onehot, count=CAMERA_PARTS):
    parts = split(terms, count)
    masked = []
    for mask in masks:
        masked.append(parts * jnp.concatenate([mask] * (parts.shape[0] // mask.shape[0]), 0))
    summed = product(jnp.concatenate(masked, 0), onehot)
    rows = parts.shape[0]
    return [sum_parts(summed[n * rows : (n + 1) * rows], count) for n in range(len(masks))]


def inverse_three(a, b, c, e, f, i):
    adjoint = [e * i - f * f, c * f - b * i, b * f - c * e, a * i - c * c, b * c - a * f, a * e - b * b]
    determinant = a * adjoint[0] + b * adjoint[1] + c * adjoint[2]
    return [entry / determinant for entry in adjoint]


def apply_three(inverse, vector):
    a, b, c, e, f, i = inverse
    x, y, z = vector
    return [a * x + b * y + c * z, b * x + e * y + f * z, c * x + f * y + i * z]


def block_inverse(entry):
    work = {(i, j): entry(i, j) for i, j in PAIRS}
    for p in range(9):
        scale = 1.0 / work[p, p]
        column = [work[max(i, p), min(i, p)] for i in range(9)]
        scaled = [value * scale for value in column]
        for i, j in PAIRS:
            if i == p and j == p:
                work[i, j] = -scale
            elif i == p:
                work[i, j] = scaled[j]
            elif j == p:
                work[i, j] = scaled[i]
            else:
                work[i, j] = work[i, j] - column[i] * scaled[j]
    return work


def inner_regions(regions):
    return max(n for n in range(1, regions + 1) if regions % n == 0 and n * n <= regions)


def kernel(
    groups,
    regions,
    cam_in,
    point_in,
    res_in,
    camera_in,
    slot_in,
    cam_step_ref,
    point_step_ref,
    cam_ref,
    point_ref,
    res_ref,
    camera_ref,
    slot_ref,
    cam_store,
    point_store,
    res_store,
    cam_hot,
    point_hot,
    stage,
    point_stage,
    near_mask,
    normal_stage,
    solve,
    normal_part,
    normal_recv,
    part,
    recv,
    table,
    first_sums,
    second_sums,
    last_sums,
    near_send,
    near_recv,
    sum_send,
    sum_recv,
    load,
):
    group = lax.axis_index("grp")
    region = lax.axis_index("reg")
    blocks = 3 * groups
    tiles = camera_ref.shape[0]

    loads = [
        pltpu.make_async_copy(source, target, load.at[n])
        for n, (source, target) in enumerate(
            [
                (camera_in, camera_ref),
                (slot_in, slot_ref),
                (cam_in, cam_ref),
                (point_in, point_ref),
                (res_in, res_ref),
            ]
        )
    ]
    for copy in loads:
        copy.start()

    def turned(position, step, size):
        return lax.select(position + step >= size, position + step - size, position + step)

    inner = inner_regions(regions)
    outer = regions // inner
    within = lax.rem(region, inner)
    plane = region // inner
    others_group = [turned(group, j, groups) for j in range(groups)]
    others_within = [turned(within, j, inner) for j in range(inner)]
    others_plane = [turned(plane, j, outer) for j in range(outer)]
    first_level = [(g, plane * inner + r) for r in others_within for g in others_group][1:]
    second_level = [(group, p * inner + within) for p in others_plane][1:]
    first_me = group * inner + within
    everyone = [(g, r) for r in [turned(region, j, regions) for j in range(regions)] for g in others_group][1:]
    me = group * regions + region

    barrier = pltpu.get_barrier_semaphore()
    for other in everyone:
        pl.semaphore_signal(barrier, inc=1, device_id=other, device_id_type=MESH)
    greeted = len(everyone)

    mine = groups + group
    has_below, has_above = region > 0, region < regions - 1

    class Near:
        def __init__(self, phase, source, target):
            self.copies = [[], [], []]
            n = 0
            for offset in range(3):
                for j in range(1 if offset == 1 else 0, groups):
                    other = others_group[j]
                    self.copies[offset].append(
                        pltpu.make_async_remote_copy(
                            src_ref=source(offset * groups + other),
                            dst_ref=target((2 - offset) * groups + group),
                            send_sem=near_send.at[phase, n],
                            recv_sem=near_recv.at[phase, n],
                            device_id=(other, turned(region, (offset - 1) % regions, regions)),
                            device_id_type=MESH,
                        )
                    )
                    n += 1

        def each(self, below, above, act):
            @pl.when(has_below)
            def _():
                for copy in self.copies[below]:
                    act(copy)

            @pl.when(has_above)
            def _():
                for copy in self.copies[above]:
                    act(copy)

            for copy in self.copies[1]:
                act(copy)

        def start(self):
            self.each(0, 2, lambda copy: copy.start())
            return self

        def wait(self):
            self.each(2, 0, lambda copy: copy.wait_recv())

        def wait_from(self, offset):
            if offset == 1:
                for copy in self.copies[1]:
                    copy.wait_recv()
                return

            @pl.when(has_below if offset == 0 else has_above)
            def _():
                for copy in self.copies[2 - offset]:
                    copy.wait_recv()

        def finish(self):
            self.each(0, 2, lambda copy: copy.wait_send())

    def clear_ends(ref):
        @pl.when(region == 0)
        def _():
            for j in range(groups):
                ref[j] = jnp.zeros(ref.shape[1:], jnp.float32)

        @pl.when(region == regions - 1)
        def _():
            for j in range(groups):
                ref[2 * groups + j] = jnp.zeros(ref.shape[1:], jnp.float32)

    def push(ref, at, others, level, phase):
        for other in others:
            pltpu.make_async_remote_copy(
                src_ref=ref.at[phase, at],
                dst_ref=ref.at[phase, at],
                send_sem=sum_send.at[level, phase],
                recv_sem=sum_recv.at[level, phase],
                device_id=other,
                device_id_type=MESH,
            ).start()

    def pulled(ref, count, level, phase):
        bytes_of = ref.at[phase, pl.ds(0, count)]
        pltpu.make_async_copy(bytes_of, bytes_of, sum_recv.at[level, phase]).wait()
        return jnp.sum(ref[phase], axis=0)

    def sum_start(phase, row):
        if phase == ITERS - 1:
            last_sums[0, me] = row
            push(last_sums, me, everyone, 2, 0)
            return
        first_sums[phase, first_me] = row
        push(first_sums, first_me, first_level, 0, phase)

    def sum_middle(phase):
        second_sums[phase, plane] = pulled(first_sums, len(first_level), 0, phase)
        push(second_sums, plane, second_level, 1, phase)

    def sum_wait(phase):
        if phase == ITERS - 1:
            sums = pulled(last_sums, len(everyone), 2, 0)
        else:
            sums = pulled(second_sums, len(second_level), 1, phase)
        return [sums[:, n : n + 1] for n in range(3)]

    def sum_finish(phase):
        levels = [(0, first_sums, first_level), (1, second_sums, second_level)]
        if phase == ITERS - 1:
            phase, levels = 0, [(2, last_sums, everyone)]
        for level, ref, others in levels:
            bytes_of = ref.at[phase, pl.ds(0, len(others))]
            pltpu.make_async_copy(bytes_of, bytes_of, sum_send.at[level, phase]).wait()

    clear_ends(normal_recv)
    for turn in range(ITERS):
        clear_ends(table.at[turn])
        clear_ends(recv.at[turn])
    stage[...] = jnp.zeros_like(stage)
    point_stage[...] = jnp.zeros_like(point_stage)
    normal_stage[...] = jnp.zeros_like(normal_stage)

    for copy in loads[:2]:
        copy.wait()
    camera = camera_ref[...]
    owner = jnp.right_shift(camera, C_DEV.bit_length() - 1)
    lane = jnp.bitwise_and(camera, C_DEV - 1)
    owner_group = jnp.zeros_like(owner)
    for j in range(1, groups):
        owner_group = owner_group + jnp.where(owner >= j * regions, 1, 0)
    offset_of = owner - owner_group * regions - region + 1
    block_of = offset_of * groups + owner_group
    for n in range(3):
        here = jnp.where(offset_of == n, 1.0, 0.0)
        for s in range(tiles):
            row = jnp.broadcast_to(here[s : s + 1], (ROWS, LANES))
            near_mask[n, :, s * LANES : (s + 1) * LANES] = row.astype(jnp.bfloat16)
    slot = slot_ref[...]
    point_lane = jnp.bitwise_and(slot, LANES - 1)
    point_tile = jnp.right_shift(slot, LANES.bit_length() - 1)

    column_t = jnp.transpose((owner_group * C_DEV + lane).astype(jnp.float32))
    cam_iota = lax.broadcasted_iota(jnp.int32, (LANES, groups * C_DEV), 1).astype(jnp.float32)
    for s in range(tiles):
        at = slice(s * LANES, (s + 1) * LANES)
        cam_hot[at, :] = jnp.where(column_t[:, s : s + 1] == cam_iota, 1.0, 0.0).astype(jnp.bfloat16)

    for copy in loads[2:]:
        copy.wait()
    for s in range(tiles):
        lanes = slice(s * LANES, (s + 1) * LANES)
        cam_store[pl.ds(s, 18, stride=tiles), :] = cam_ref[:, lanes].astype(jnp.float32)
        point_store[pl.ds(s, 6, stride=tiles), :] = point_ref[:, lanes].astype(jnp.float32)
        res_store[pl.ds(s, 2, stride=tiles), :] = res_ref[:, lanes]
    cam_rows = [cam_store[n * tiles : (n + 1) * tiles] for n in range(18)]
    point_rows = [point_store[n * tiles : (n + 1) * tiles] for n in range(6)]
    residuals = [res_store[n * tiles : (n + 1) * tiles] for n in range(2)]

    def put(ref, row, term):
        ref[pl.ds(row, tiles, stride=ref.shape[0] // tiles), :] = term

    def staged(ref):
        rows = ref.shape[0] // tiles
        return jnp.concatenate([ref[s * rows : (s + 1) * rows] for s in range(tiles)], 1)

    def pick(rows, tile, at):
        total = None
        for n, row in enumerate(rows):
            wide = jnp.broadcast_to(row, (tiles, LANES))
            got = jnp.take_along_axis(wide, at, axis=1, mode="promise_in_bounds")
            total = got if total is None else jnp.where(tile == n, got, total)
        return total

    def point_terms(values, stage):
        for j in range(3):
            put(stage, j, point_rows[j] * values[0] + point_rows[3 + j] * values[1])

    masks = [near_mask.at[n] for n in range(3)]

    def by_block(ref, summed):
        for n in range(3):
            for j in range(groups):
                ref[n * groups + j] = summed[n][:, j * C_DEV : (j + 1) * C_DEV]

    def rows_of(block, count):
        return [block[j : j + 1] for j in range(count)]

    def remains(values, gathered):
        solved = apply_three(inverse, rows_of(gathered, 3))
        picked = [
            pick([row[:, n * LANES : (n + 1) * LANES] for n in range(P_DEV // LANES)], point_tile, point_lane)
            for row in solved
        ]
        return [
            values[i]
            - (
                point_rows[3 * i] * picked[0]
                + point_rows[3 * i + 1] * picked[1]
                + point_rows[3 * i + 2] * picked[2]
            )
            for i in range(2)
        ]

    for n, (i, j) in enumerate(PAIRS):
        put(normal_stage, n, cam_rows[i] * cam_rows[j] + cam_rows[9 + i] * cam_rows[9 + j])
    by_block(
        normal_part,
        sum_near(staged(normal_stage), [mask[...] for mask in masks], cam_hot[...]),
    )
    pl.semaphore_wait(barrier, greeted)
    normal = Near(0, lambda block: normal_part.at[block], lambda at: normal_recv.at[at]).start()
    normal_recv[mine] = normal_part[mine]

    slot_t = jnp.transpose(slot.astype(jnp.float32))
    point_iota = lax.broadcasted_iota(jnp.int32, (LANES, P_DEV), 1).astype(jnp.float32)
    for s in range(tiles):
        at = slice(s * LANES, (s + 1) * LANES)
        point_hot[at, :] = jnp.where(slot_t[:, s : s + 1] == point_iota, 1.0, 0.0).astype(jnp.bfloat16)
    first = [residuals[0], residuals[1]]
    point_terms(first, stage)
    for n, (i, j) in enumerate([(0, 0), (0, 1), (0, 2), (1, 1), (1, 2), (2, 2)]):
        put(stage, 3 + n, point_rows[i] * point_rows[j] + point_rows[3 + i] * point_rows[3 + j])
    sums = sum_into(staged(stage), point_hot[...])
    entries = rows_of(sums[3:9], 6)
    for n in (0, 3, 5):
        entries[n] = entries[n] + DAMPING
    inverse = inverse_three(*entries)
    point_total = sums[:8]

    def send_back(phase, at, remain):
        for k in range(9):
            put(stage, k, cam_rows[k] * remain[0] + cam_rows[9 + k] * remain[1])
        by_block(part.at[at], sum_near(staged(stage), [mask[...] for mask in masks], cam_hot[...]))
        back = Near(
            phase, lambda block: part.at[at, block, pl.ds(0, 9)], lambda block: recv.at[at, block]
        ).start()
        recv[at, mine] = part[at, mine, :9]
        return back

    def taken_back(at):
        out = recv[at, 0]
        for n in range(1, blocks):
            out = out + recv[at, n]
        return out

    gradient = send_back(1, ITERS - 1, remains(first, sums))
    normal.wait()
    total = normal_recv[0]
    for n in range(1, blocks):
        total = total + normal_recv[n]

    def entry(i, j):
        n = PAIRS.index((i, j))
        row = total[n : n + 1]
        return row + DAMPING if i == j else row

    minus_inverse = block_inverse(entry)
    for i, j in PAIRS:
        solve[i, j : j + 1, :] = -minus_inverse[i, j]
        if i != j:
            solve[j, i : i + 1, :] = -minus_inverse[i, j]

    def precondition(field):
        out = solve[0] * field[0:1]
        for k in range(1, 9):
            out = out + solve[k] * field[k : k + 1]
        return out

    def dot(x, y):
        return jnp.sum(x * y, axis=0, keepdims=True)

    def moved(x, scale, y):
        return [a + scale * b for a, b in zip(x, y)]

    gradient.wait()
    exchanges = [normal, gradient]
    lanes_of = lax.broadcasted_iota(jnp.int32, (1, LANES), 1)
    residual = -taken_back(ITERS - 1)
    field = precondition(residual)
    cam_step = jnp.zeros((9, C_DEV), jnp.float32)
    z = direction = slope = image = product = current = curvature = None
    for turn in range(ITERS):
        table[turn, mine] = field
        spread = Near(
            2 + 2 * turn, lambda block: table.at[turn, mine], lambda at: table.at[turn, at]
        ).start()
        exchanges.append(spread)
        if turn > 0:
            sum_middle(turn - 1)
        picked = [None] * 9
        for offset in (1, 0, 2):
            spread.wait_from(offset)
            for n in range(offset * groups, (offset + 1) * groups):
                for k in range(9):
                    row = jnp.broadcast_to(table[turn, n, k : k + 1], (tiles, LANES))
                    got = jnp.take_along_axis(row, lane, axis=1, mode="promise_in_bounds")
                    picked[k] = got if picked[k] is None else jnp.where(block_of == n, got, picked[k])
        if turn > 0:
            following, energy, cross = sum_wait(turn - 1)
        values = [None, None]
        for k in range(9):
            for i in range(2):
                term = cam_rows[9 * i + k] * picked[k]
                values[i] = term if k == 0 else values[i] + term
        point_terms(values, point_stage)
        fresh = [field] + values + [sum_into(staged(point_stage), point_hot[...], POINT_PARTS)]
        if turn == 0:
            z = fresh
        else:
            if turn == 1:
                curvature, direction, slope, image = energy, [z[0], z[3]], fresh, product
            else:
                ratio = following / current
                curvature = energy + ratio * (2.0 * cross + ratio * curvature)
                direction = moved([z[0], z[3]], ratio, direction)
                slope = moved(fresh, ratio, slope)
                image = product + ratio * image
            current = following
            step_size = current / curvature
            cam_step = cam_step + step_size * direction[0]
            point_total = point_total + step_size * direction[1]
            residual = residual - step_size * image
            z = moved(z, -step_size, slope)
        remain = remains(z[1:3], z[3])
        if turn + 1 < ITERS:
            back = send_back(3 + 2 * turn, turn, remain)
            exchanges.append(back)
        sums_of = [
            dot(residual, z[0]),
            DAMPING * dot(z[0], z[0]) + dot(z[1], remain[0]) + dot(z[2], remain[1]),
            jnp.zeros((1, LANES), jnp.float32) if turn == 0 else dot(z[0], image),
        ]
        sums_of = [jnp.sum(x, axis=1, keepdims=True) for x in sums_of]
        sum_start(turn, jnp.where(lanes_of == 0, sums_of[0], jnp.where(lanes_of == 1, sums_of[1], sums_of[2])))
        if turn + 1 < ITERS:
            back.wait()
            product = DAMPING * z[0] + taken_back(turn)
            field = precondition(product)

    for exchange in exchanges:
        exchange.finish()
    for turn in range(ITERS - 1):
        sum_finish(turn)
    following, energy, cross = sum_wait(ITERS - 1)
    ratio = following / current
    curvature = energy + ratio * (2.0 * cross + ratio * curvature)
    direction = moved([z[0], z[3]], ratio, direction)
    step_size = following / curvature
    cam_step = cam_step + step_size * direction[0]
    point_total = point_total + step_size * direction[1]
    sum_finish(ITERS - 1)
    cam_step_ref[...] = cam_step
    for j, row in enumerate(apply_three(inverse, rows_of(point_total, 3))):
        point_step_ref[j : j + 1, :] = -row


def local(groups, regions, cam_jacobian, point_jacobian, residuals, obs_camera, obs_point):
    count = obs_camera.shape[0]
    tiles = count // LANES
    blocks = 3 * groups
    inner = inner_regions(regions)
    phases = 2 * ITERS + 1
    groups_wide = groups * C_DEV
    f32, bf16 = jnp.float32, jnp.bfloat16
    near = blocks - 1
    return pl.pallas_call(
        functools.partial(kernel, groups, regions),
        out_shape=(
            jax.ShapeDtypeStruct((9, C_DEV), f32),
            jax.ShapeDtypeStruct((3, P_DEV), f32),
        ),
        in_specs=[pl.BlockSpec(memory_space=pltpu.HBM)] * 5,
        out_specs=[pl.BlockSpec(memory_space=pltpu.VMEM)] * 2,
        scratch_shapes=[
            pltpu.VMEM(cam_jacobian.shape, bf16),
            pltpu.VMEM(point_jacobian.shape, bf16),
            pltpu.VMEM(residuals.shape, f32),
            pltpu.VMEM((tiles, LANES), jnp.int32),
            pltpu.VMEM((tiles, LANES), jnp.int32),
            pltpu.VMEM((18 * tiles, LANES), f32),
            pltpu.VMEM((6 * tiles, LANES), f32),
            pltpu.VMEM((2 * tiles, LANES), f32),
            pltpu.VMEM((count, groups_wide), bf16),
            pltpu.VMEM((count, P_DEV), bf16),
            pltpu.VMEM((tiles * ROWS, LANES), f32),
            pltpu.VMEM((tiles * 8, LANES), f32),
            pltpu.VMEM((3, ROWS, count), bf16),
            pltpu.VMEM((tiles * NORMAL_ROWS, LANES), f32),
            pltpu.VMEM((9, 9, C_DEV), f32),
            pltpu.VMEM((blocks, NORMAL_ROWS, C_DEV), f32),
            pltpu.VMEM((blocks, NORMAL_ROWS, C_DEV), f32),
            pltpu.VMEM((ITERS, blocks, ROWS, C_DEV), f32),
            pltpu.VMEM((ITERS, blocks, 9, C_DEV), f32),
            pltpu.VMEM((ITERS, blocks, 9, C_DEV), f32),
            pltpu.VMEM((ITERS - 1, groups * inner, 1, LANES), f32),
            pltpu.VMEM((ITERS - 1, regions // inner, 1, LANES), f32),
            pltpu.VMEM((1, groups * regions, 1, LANES), f32),
            pltpu.SemaphoreType.DMA((phases, near)),
            pltpu.SemaphoreType.DMA((phases, near)),
            pltpu.SemaphoreType.DMA((3, ITERS)),
            pltpu.SemaphoreType.DMA((3, ITERS)),
            pltpu.SemaphoreType.DMA((5,)),
        ],
        compiler_params=pltpu.CompilerParams(
            collective_id=0, has_side_effects=True, vmem_limit_bytes=56 * 1024 * 1024
        ),
    )(
        cam_jacobian,
        point_jacobian,
        residuals,
        obs_camera.reshape(tiles, LANES),
        obs_point.reshape(tiles, LANES),
    )


def solution(mesh):
    placed = (
        P(None, ("grp", "reg")),
        P(None, ("grp", "reg")),
        P(None, ("grp", "reg")),
        P(("grp", "reg")),
        P(("grp", "reg")),
    )
    return jax.shard_map(
        functools.partial(local, mesh.shape["grp"], mesh.shape["reg"]),
        mesh=mesh,
        in_specs=placed,
        out_specs=(P(None, ("grp", "reg")), P(None, ("grp", "reg"))),
        check_vma=False,
    )
```
